128 devices in a mesh: grp: 8 (over y, x_lo), tp: 16 (over z, x_hi, core).
Axes of the slice: x: 4 (x_hi: 2, x_lo: 2; x = x_hi * 2 + x_lo), y: 4, z: 4, core: 2. Of those that a mesh axis runs over, the one named last changes fastest.
Arguments:
- low_state: bfloat16 [16384, 16384], P('grp', 'tp'), may hold values from -6 to 6
- mid_state: bfloat16 [16384, 16384], P('grp', 'tp'), may hold values from -6 to 6
- high_state: bfloat16 [16384, 16384], P('grp', 'tp'), may hold values from -6 to 6
- w_low: bfloat16 [16384, 1024], P('tp', 'grp'), may hold values from -0.02734375 to 0.02734375
- w_mid: bfloat16 [16384, 1024], P('tp', 'grp'), may hold values from -0.02734375 to 0.02734375
- w_high: bfloat16 [16384, 1024], P('tp', 'grp'), may hold values from -0.02734375 to 0.02734375
- kv_grad: bfloat16 [16384, 1024], P(('grp', 'tp')), may hold values from -24 to 24
- loss_mask: int32 [16384], P(('grp', 'tp')), may hold values 0 or 1
Outputs:
- keys_values: bfloat16 [16384, 1024], P(('grp', 'tp'))
- grad_low: bfloat16 [16384, 1024], P('tp', 'grp')
- grad_mid: bfloat16 [16384, 1024], P('tp', 'grp')
- grad_high: bfloat16 [16384, 1024], P('tp', 'grp')
The draws below stay inside these ranges and needn't reach their ends.
All inputs are finite; a program needn't handle non-finite values. No bound on the sum of `loss_mask` on one device may be relied on, other than what follows from the above.
Results may differ from the reference program's by a relative error of at most 0.019.
Values may be sent and summed in bfloat16 or wider, within the bound.
No kernel may reach another device: no remote copies, remote signals or barrier semaphores. Data moves between devices by JAX's collectives and lax.ppermute only.
A program may use at most 128 MiB of HBM per device.

```python
import jax
import jax.numpy as jnp
from jax import lax

D = 16384
KVW = 1024
TOK_G = 2048
TOKENS = 16384
N_GRP = 8


def place_ends(array, key, smallest, top_value):
    place = [jax.random.randint(jax.random.fold_in(key, axis), (), 0, length) for axis, length in enumerate(array.shape)]
    main_axis = array.shape.index(max(array.shape))
    beside = place[:main_axis] + [(place[main_axis] + 1) % array.shape[main_axis]] + place[main_axis + 1:]
    return array.at[tuple(place)].set(smallest).at[tuple(beside)].set(top_value)


def with_spikes(entries, own_key, source, target, parts, factor):
    def block_of(position):
        return (jnp.arange(entries.shape[position]) // (entries.shape[position] // parts)).reshape((-1,) + (1,) * (entries.ndim - 1 - position))

    near = jax.random.permutation(own_key, parts)[block_of(target)]
    second = (block_of(target) + parts // 2) % parts
    return jnp.where((block_of(source) == near) | (block_of(source) == second), factor * entries, entries)


def shard_levels(key, dims, shards, smallest, high):
    def one(axis_at, shards_of):
        heights = jax.random.uniform(jax.random.fold_in(jax.random.fold_in(key, 6), axis_at), (shards_of,), jnp.float32, smallest / len(shards), high / len(shards))
        return jnp.repeat(jnp.exp(heights), dims[axis_at] // shards_of).reshape((-1,) + (1,) * (len(dims) - axis_at - 1))

    level = one(*shards[0])
    for cut in shards[1:]:
        level = level * one(*cut)
    return level


def scatter_about(key, shape, width, bound, pieces=(), dtype=jnp.bfloat16):
    array = jax.random.normal(key, shape, jnp.float32) * width
    if len(pieces) > 0:
        array = shard_levels(key, shape, pieces, -0.22, 0.18) * array
    return jnp.clip(array, min=-bound, max=bound).astype(dtype)


def gaussian_with(own_key, extent, deviation, reach, split, heavy, kind=jnp.bfloat16):
    result = deviation * jax.random.normal(own_key, extent, jnp.float32)
    if split:
        result = result * shard_levels(own_key, extent, split, -0.22, 0.18)
    return jnp.clip(with_spikes(result, jax.random.fold_in(own_key, 3), *heavy), -reach, reach).astype(kind)


def setup_inputs(seed: int = 0) -> dict:
    arg_keys = jax.random.split(jax.random.key(seed), 9)
    return {
        "low_state": scatter_about(arg_keys[0], (TOKENS, D), 1.0, 6.0, ((0, 8), (1, 16))),
        "mid_state": scatter_about(arg_keys[1], (TOKENS, D), 1.0, 6.0, ((0, 8), (1, 16))),
        "high_state": scatter_about(arg_keys[2], (TOKENS, D), 1.0, 6.0, ((0, 8), (1, 16))),
        "w_low": scatter_about(arg_keys[3], (D, KVW), (3 * D) ** -0.5, 0.02734375, ((0, 16), (1, 8))),
        "w_mid": scatter_about(arg_keys[4], (D, KVW), (3 * D) ** -0.5, 0.02734375, ((0, 16), (1, 8))),
        "w_high": scatter_about(arg_keys[5], (D, KVW), (3 * D) ** -0.5, 0.02734375, ((0, 16), (1, 8))),
        "kv_grad": gaussian_with(arg_keys[6], (TOKENS, KVW), 1.0, 24.0, ((0, 128),), (0, 1, 128, 5.5)),
        "loss_mask": place_ends((jax.random.randint(arg_keys[7], (TOKENS,), 0, 8) < 7).astype(jnp.int32), jax.random.fold_in(arg_keys[7], 1), 0, 1),
    }


def reference(low_state, mid_state, high_state, w_low, w_mid, w_high, kv_grad, loss_mask):
    joined = jnp.dot(low_state, w_low, preferred_element_type=jnp.float32)
    joined = joined + jnp.dot(mid_state, w_mid, preferred_element_type=jnp.float32)
    joined = joined + jnp.dot(high_state, w_high, preferred_element_type=jnp.float32)
    keys_values = joined.astype(jnp.bfloat16)
    masked = (kv_grad.astype(jnp.float32) * loss_mask.astype(jnp.float32)[:, None]).astype(jnp.bfloat16)
    scale = TOKENS ** -0.5
    results = []
    for state in (low_state, mid_state, high_state):
        total = jnp.zeros((D, KVW), jnp.float32)
        for group in range(N_GRP):
            rows = state[group * TOK_G:(group + 1) * TOK_G]
            block = masked[group * TOK_G:(group + 1) * TOK_G]
            part = jnp.dot(rows.T, block, preferred_element_type=jnp.float32) * scale
            total = total + lax.optimization_barrier(part.astype(jnp.bfloat16)).astype(jnp.float32)
        results.append(total.astype(jnp.bfloat16))
    return (keys_values, results[0], results[1], results[2])
```

```python
import jax
import jax.numpy as jnp
from jax import lax
from jax.experimental import pallas as pl
from jax.experimental.pallas import tpu as pltpu
from jax.sharding import PartitionSpec as P

BF = jnp.bfloat16
F32 = jnp.float32
VMEM_LIMIT = 48 * 1024 * 1024
GRP, TP = 8, 16
FULL = ("grp", "tp")


def full_perm(move):
    pairs = []
    for g in range(GRP):
        for t in range(TP):
            y, xl, z, xh, c = move(g // 2, g % 2, t // 4, t // 2 % 2, t % 2)
            pairs.append((g * TP + t, (y % 4 * 2 + xl % 2) * TP + z % 4 * 4 + xh % 2 * 2 + c % 2))
    return pairs


Y1 = full_perm(lambda y, xl, z, xh, c: (y + 1 - 2 * c, xl, z, xh, c))
Y2 = full_perm(lambda y, xl, z, xh, c: (y - 1 + 2 * c, xl, z, xh, c))
Z1 = full_perm(lambda y, xl, z, xh, c: (y, xl, z + 1 - 2 * c, xh, c))
Z2 = full_perm(lambda y, xl, z, xh, c: (y, xl, z - 1 + 2 * c, xh, c))
XL = full_perm(lambda y, xl, z, xh, c: (y, xl + 1, z, xh, c))
XH = full_perm(lambda y, xl, z, xh, c: (y, xl, z, xh + 1, c))
CORE = full_perm(lambda y, xl, z, xh, c: (y, xl, z, xh, c + 1))


def send(array, pairs):
    return lax.ppermute(array, FULL, pairs)


def add(*arrays):
    total = arrays[0].astype(F32)
    for array in arrays[1:]:
        total = total + array.astype(F32)
    return total.astype(BF)


def place():
    g = lax.axis_index("grp")
    t = lax.axis_index("tp")
    c = t % 2
    return g // 2, g % 2, t // 4, t // 2 % 2, c, 1 - 2 * c


def params():
    return pltpu.CompilerParams(vmem_limit_bytes=VMEM_LIMIT)


def whole(*shape):
    return pl.BlockSpec(shape, lambda *_: (0,) * len(shape))


def mask_kernel(grad_ref, mask_ref, out_ref):
    turned = grad_ref[...].astype(F32).T
    out_ref[...] = (turned * mask_ref[...].astype(F32)).astype(BF)


def masked_turned(kv_grad, loss_mask):
    rows, cols = kv_grad.shape
    return pl.pallas_call(
        mask_kernel,
        out_shape=jax.ShapeDtypeStruct((cols, rows), BF),
        compiler_params=params(),
        cost_estimate=pl.CostEstimate(flops=rows * cols, bytes_accessed=4 * rows * cols, transcendentals=0),
        name="masked",
    )(kv_grad, loss_mask.reshape(1, rows))


def forward_kernel(s0, s1, s2, w0, w1, w2, w3, even_ref, odd_ref, w_all):
    @pl.when(pl.program_id(0) == 0)
    def _():
        c = lax.axis_index("tp") % 2
        for i, w in ((0, w0), (1, w1), (2 + c, w2), (3 - c, w3)):
            w_all[:, pl.ds(pl.multiple_of(i * 128, 128), 128)] = w[...]

    depth = s0.shape[1]
    total = jnp.dot(s0[...], w_all[0:depth, :], preferred_element_type=F32)
    total += jnp.dot(s1[...], w_all[depth:2 * depth, :], preferred_element_type=F32)
    total += jnp.dot(s2[...], w_all[2 * depth:3 * depth, :], preferred_element_type=F32)
    total = total.astype(BF)
    mine = lax.axis_index("tp") % 2 == 0
    for h in range(2):
        first = total[h * 256:h * 256 + 128]
        second = total[h * 256 + 128:h * 256 + 256]
        even_ref[0, h] = jnp.where(mine, first, second)
        odd_ref[0, h] = jnp.where(mine, second, first)


def forward(states, blocks):
    tokens, depth = states[0].shape
    cols = 128 * len(blocks)
    state_spec = pl.BlockSpec((512, depth), lambda i: (i, 0))
    out_spec = pl.BlockSpec((1, 2, 128, cols), lambda i: (i, 0, 0, 0))
    out = jax.ShapeDtypeStruct((4, 2, 128, cols), BF)
    return pl.pallas_call(
        forward_kernel,
        grid=(4,),
        in_specs=[state_spec] * 3 + [whole(3 * depth, 128)] * 4,
        out_specs=[out_spec, out_spec],
        out_shape=[out, out],
        scratch_shapes=[pltpu.VMEM((3 * depth, cols), BF)],
        compiler_params=params(),
        cost_estimate=pl.CostEstimate(
            flops=6 * tokens * depth * cols, bytes_accessed=6 * tokens * depth + 8 * depth * cols, transcendentals=0
        ),
        name="forward",
    )(*states, *blocks)


def backward_kernel(other, m0, m1, m2, m3, s0, s1, s2, p2, pm, pp, p0, turned):
    y, xl, z, xh, c, d = place()
    half = (xl + 1) % 2 if other else xl

    @pl.when(pl.program_id(0) == 0)
    def _():
        for ref, flip, second in ((m0, 0, 0), (m1, 1, 0), (m2, 0, 1), (m3, 1, 1)):
            core = (c + flip) % 2
            way = 1 - 2 * core
            if second:
                spots = ((z + 2, xh), (z - way, xh + 1), (z + way, xh + 1), (z + 2, xh + 1))
            else:
                spots = ((z, xh), (z - way, xh), (z + way, xh), (z, xh + 1))
            for j, (zz, hh) in enumerate(spots):
                token = (zz + 4) % 4 * 4 + hh % 2 * 2 + core
                lanes = pl.ds(pl.multiple_of(token * 128, 128), 128)
                for r, yy in enumerate((y + 2, y - d, y + d, y)):
                    rows = pl.ds(pl.multiple_of(((yy + 4) % 4 * 2 + half) * 128, 128), 128)
                    turned[r * 128:(r + 1) * 128, lanes] = ref[j, rows, :]

    for s, state in enumerate((s0, s1, s2)):
        product = jnp.dot(turned[...], state[...], preferred_element_type=F32) * (16384 ** -0.5)
        product = product.astype(BF)
        for r, out in enumerate((p2, pm, pp, p0)):
            out[s] = product[r * 128:(r + 1) * 128]


def backward(states, masked, other):
    tokens, depth = states[0].shape
    tile = 256
    out_spec = pl.BlockSpec((3, 128, tile), lambda i: (0, 0, i))
    out = jax.ShapeDtypeStruct((3, 128, depth), BF)

    def kernel(*refs):
        backward_kernel(other, *refs)

    return pl.pallas_call(
        kernel,
        grid=(depth // tile,),
        in_specs=[whole(*masked[0].shape)] * 4 + [pl.BlockSpec((tokens, tile), lambda i: (0, i))] * 3,
        out_specs=[out_spec] * 4,
        out_shape=[out] * 4,
        scratch_shapes=[pltpu.VMEM((512, tokens), BF)],
        compiler_params=params(),
        cost_estimate=pl.CostEstimate(
            flops=6 * tokens * depth * 512, bytes_accessed=6 * tokens * depth + 16 * tokens * 256, transcendentals=0
        ),
        name="backward_other" if other else "backward_own",
    )(*masked, *states)


def pick_kernel(mine, theirs, q2, qm, qp, q0):
    _, _, z, _, _, d = place()
    for out, zz in ((q2, z + 2), (qm, z - d), (qp, z + d), (q0, z)):
        k = (zz + 4) % 4
        out[...] = (mine[k].astype(F32) + theirs[k].astype(F32)).astype(BF)


def pick(mine, theirs):
    out = jax.ShapeDtypeStruct(mine.shape[1:], BF)
    return pl.pallas_call(
        pick_kernel,
        out_shape=[out] * 4,
        compiler_params=params(),
        cost_estimate=pl.CostEstimate(flops=mine.size, bytes_accessed=6 * mine.size, transcendentals=0),
        name="pick",
    )(mine, theirs)


def split_kernel(a, b, c, mine, theirs):
    h = lax.axis_index("tp") // 2 % 2
    for out, k in ((mine, h), (theirs, (h + 1) % 2)):
        out[...] = (a[k].astype(F32) + b[k].astype(F32) + c[k].astype(F32)).astype(BF)


def split(a, b, c):
    out = jax.ShapeDtypeStruct(a.shape[1:], BF)
    return pl.pallas_call(
        split_kernel,
        out_shape=[out] * 2,
        compiler_params=params(),
        cost_estimate=pl.CostEstimate(flops=2 * a.size, bytes_accessed=8 * a.size, transcendentals=0),
        name="split",
    )(a, b, c)


def join_kernel(a0, b0, a1, b1, out):
    y, xl, _, _, _, _ = place()
    first = ((y, xl), (y, xl + 1), (y - 1, xl), (y + 1, xl))
    second = ((y + 2, xl), (y + 2, xl + 1), (y - 1, xl + 1), (y + 1, xl + 1))
    for a, b, spots in ((a0, b0, first), (a1, b1, second)):
        for j, (yy, hh) in enumerate(spots):
            lanes = pl.ds(pl.multiple_of(((yy + 4) % 4 * 2 + hh % 2) * 128, 128), 128)
            cut = slice(j * 128, (j + 1) * 128)
            out[:, lanes] = (a[:, cut].astype(F32) + b[:, cut].astype(F32)).astype(BF)


def join(a0, b0, a1, b1):
    rows, cols = a0.shape
    return pl.pallas_call(
        join_kernel,
        out_shape=jax.ShapeDtypeStruct((rows, 2 * cols), BF),
        compiler_params=params(),
        cost_estimate=pl.CostEstimate(flops=2 * a0.size, bytes_accessed=12 * a0.size, transcendentals=0),
        name="join",
    )(a0, b0, a1, b1)


def finish_kernel(a, b, c, e, g0, g1, g2):
    for s, out in enumerate((g0, g1, g2)):
        total = a[s].astype(F32) + b[s].astype(F32) + c[s].astype(F32) + e[s].astype(F32)
        out[...] = total.T.astype(BF)


def finish(a, b, c, e):
    _, cols, depth = a.shape
    return pl.pallas_call(
        finish_kernel,
        out_shape=[jax.ShapeDtypeStruct((depth, cols), BF)] * 3,
        compiler_params=params(),
        cost_estimate=pl.CostEstimate(flops=4 * a.size, bytes_accessed=10 * a.size, transcendentals=0),
        name="finish",
    )(a, b, c, e)


def scatter_tokens(mine, theirs):
    theirs = send(theirs, CORE)
    q2, qm, qp, q0 = pick(mine, theirs)
    t3 = send(q2, Z2)
    t2 = send(qp, Z1)
    t1 = send(add(qm, t3), Z2)
    kept, given = split(q0, t1, t2)
    return kept, send(given, XH)


def body(low_state, mid_state, high_state, w_low, w_mid, w_high, kv_grad, loss_mask):
    states = (low_state, mid_state, high_state)
    w = jnp.concatenate((w_low, w_mid, w_high), axis=0)
    mt = masked_turned(kv_grad, loss_mask)

    x1 = send(w, XL)
    a1 = send(w, Y1)
    a2 = send(w, Y2)
    m_h = send(mt, XH)
    m_1 = send(mt, Z1)
    m_2 = send(mt, Z2)
    m_3 = send(m_1, Z1)
    h_1 = send(m_h, Z1)
    h_2 = send(m_h, Z2)
    h_3 = send(h_1, Z1)
    near = jnp.stack((mt, m_1, m_2, m_h))
    near_other = send(near, CORE)
    far = jnp.stack((m_3, h_1, h_2, h_3))
    far_other = send(far, CORE)
    masked = (near, near_other, far, far_other)

    a3 = send(a1, Y1)
    b1 = send(x1, Y1)
    b2 = send(x1, Y2)
    b3 = send(a3, XL)

    mine, theirs = forward(states, (w, x1, a1, a2))
    kept_a, got_a = scatter_tokens(mine, theirs)

    p2x, pmx, ppx, p0x = backward(states, masked, True)
    e1 = send(p2x, XL)
    e2 = send(pmx, Y2)
    e3 = send(ppx, Y1)
    p2, pm, pp, p0 = backward(states, masked, False)
    f3 = send(add(p2, e1), Y2)
    f2 = send(pp, Y1)
    fx = send(add(p0x, e2, e3), XL)
    f1 = send(add(pm, f3), Y2)

    mine, theirs = forward(states, (a3, b3, b1, b2))
    kept_b, got_b = scatter_tokens(mine, theirs)

    keys_values = join(kept_a, got_a, kept_b, got_b)
    return (keys_values, *finish(p0, fx, f1, f2))


def solution(mesh):
    in_specs = (
        P("grp", "tp"),
        P("grp", "tp"),
        P("grp", "tp"),
        P("tp", "grp"),
        P("tp", "grp"),
        P("tp", "grp"),
        P(("grp", "tp"), None),
        P(("grp", "tp")),
    )
    out_specs = (P(("grp", "tp"), None), P("tp", "grp"), P("tp", "grp"), P("tp", "grp"))
    return jax.shard_map(body, mesh=mesh, in_specs=in_specs, out_specs=out_specs, check_vma=False)
```

```python
import jax
import jax.numpy as jnp
from jax import lax
from jax.experimental import pallas as pl
from jax.experimental.pallas import tpu as pltpu
from jax.sharding import PartitionSpec as P

BF = jnp.bfloat16
F32 = jnp.float32
MIB = 1024 * 1024
LOAD_MIB = 38
GRP, TP = 8, 16
CHEAP = 1000
FULL = ("grp", "tp")


def full_perm(move):
    pairs = []
    for g in range(GRP):
        for t in range(TP):
            y, xl, z, xh, c = move(g // 2, g % 2, t // 4, t // 2 % 2, t % 2)
            pairs.append((g * TP + t, (y % 4 * 2 + xl % 2) * TP + z % 4 * 4 + xh % 2 * 2 + c % 2))
    return pairs


Y1 = full_perm(lambda y, xl, z, xh, c: (y + 1 - 2 * c, xl, z, xh, c))
Y2 = full_perm(lambda y, xl, z, xh, c: (y - 1 + 2 * c, xl, z, xh, c))
Z1 = full_perm(lambda y, xl, z, xh, c: (y, xl, z + 1 - 2 * c, xh, c))
Z2 = full_perm(lambda y, xl, z, xh, c: (y, xl, z - 1 + 2 * c, xh, c))
XL = full_perm(lambda y, xl, z, xh, c: (y, xl + 1, z, xh, c))
XH = full_perm(lambda y, xl, z, xh, c: (y, xl, z, xh + 1, c))
CORE = full_perm(lambda y, xl, z, xh, c: (y, xl, z, xh, c + 1))


def send(array, pairs):
    return lax.ppermute(array, FULL, pairs)


def add(*arrays):
    total = arrays[0].astype(F32)
    for array in arrays[1:]:
        total = total + array.astype(F32)
    return total.astype(BF)


def place():
    g = lax.axis_index("grp")
    t = lax.axis_index("tp")
    c = t % 2
    return g // 2, g % 2, t // 4, t // 2 % 2, c, 1 - 2 * c


def params(mib=8):
    return pltpu.CompilerParams(vmem_limit_bytes=mib * MIB)


def cost(flops, bytes_accessed):
    return pl.CostEstimate(flops=flops // CHEAP, bytes_accessed=bytes_accessed // CHEAP, transcendentals=0)


def fence(*arrays):
    return lax.optimization_barrier(arrays)


VMEM = pl.BlockSpec(memory_space=pltpu.VMEM)


def collect_kernel(w0, w1, w2, w_ref, sems):
    depth = w0.shape[0]
    moves = []
    for i, w in enumerate((w0, w1, w2)):
        moves.append(pltpu.make_async_copy(w, w_ref.at[pl.ds(i * depth, depth), :], sems.at[i]))
    for move in moves:
        move.start()
    for move in moves:
        move.wait()


def collect(weights):
    depth, width = weights[0].shape
    return pl.pallas_call(
        collect_kernel,
        in_specs=[pl.BlockSpec(memory_space=pl.ANY)] * 3,
        out_specs=VMEM,
        out_shape=jax.ShapeDtypeStruct((3 * depth, width), BF),
        scratch_shapes=[pltpu.SemaphoreType.DMA((3,))],
        compiler_params=params(60),
        cost_estimate=cost(0, 12 * depth * width),
        name="collect",
    )(*weights)


def mask_kernel(grad_ref, mask_ref, turned_ref, grad, mask, sems):
    moves = [
        pltpu.make_async_copy(mask_ref, mask, sems.at[0]),
        pltpu.make_async_copy(grad_ref, grad, sems.at[1]),
    ]
    for move in moves:
        move.start()
    for move in moves:
        move.wait()
    turned_ref[...] = (grad[...].astype(F32).T * mask[...].astype(F32)).astype(BF)


def masked_turned(kv_grad, loss_mask):
    rows, cols = kv_grad.shape
    return pl.pallas_call(
        mask_kernel,
        in_specs=[pl.BlockSpec(memory_space=pl.ANY)] * 2,
        out_specs=VMEM,
        out_shape=jax.ShapeDtypeStruct((cols, rows), BF),
        scratch_shapes=[
            pltpu.VMEM((rows, cols), BF),
            pltpu.VMEM((1, rows), jnp.int32),
            pltpu.SemaphoreType.DMA((2,)),
        ],
        compiler_params=params(60),
        cost_estimate=cost(rows * cols, 4 * rows * cols),
        name="masked",
    )(kv_grad, loss_mask.reshape(1, rows))


def load_kernel(*refs):
    half = len(refs) // 2
    sems = refs[-1]
    moves = [pltpu.make_async_copy(refs[i], refs[half + i], sems.at[i]) for i in range(half)]
    for move in moves:
        move.start()
    for move in moves:
        move.wait()


def load(*arrays):
    count = len(arrays)
    return pl.pallas_call(
        load_kernel,
        in_specs=[pl.BlockSpec(memory_space=pl.ANY)] * count,
        out_specs=[VMEM] * count,
        out_shape=[jax.ShapeDtypeStruct(a.shape, BF) for a in arrays],
        scratch_shapes=[pltpu.SemaphoreType.DMA((count,))],
        compiler_params=params(LOAD_MIB),
        cost_estimate=cost(0, 4 * sum(a.size for a in arrays)),
        name="load",
    )(*arrays)


def forward_kernel(swap, s0, s1, s2, wa, wb, mine_ref, theirs_ref, w_all):
    c = lax.axis_index("tp") % 2
    for i, w in ((c, wa), (1 - c, wb)) if swap else ((0, wa), (1, wb)):
        w_all[:, pl.ds(pl.multiple_of(i * 128, 128), 128)] = w[...]
    depth = s0.shape[1]
    total = jnp.dot(s0[...], w_all[0:depth, :], preferred_element_type=F32)
    total += jnp.dot(s1[...], w_all[depth:2 * depth, :], preferred_element_type=F32)
    total += jnp.dot(s2[...], w_all[2 * depth:3 * depth, :], preferred_element_type=F32)
    total = total.astype(BF)
    for z in range(4):
        for h in range(2):
            at = (z * 2 + h) * 256
            first = total[at:at + 128]
            second = total[at + 128:at + 256]
            mine_ref[z, h] = jnp.where(c == 0, first, second)
            theirs_ref[z, h] = jnp.where(c == 0, second, first)


def forward(states, blocks, swap):
    tokens, depth = states[0].shape
    out = jax.ShapeDtypeStruct((4, 2, 128, 256), BF)

    def kernel(*refs):
        forward_kernel(swap, *refs)

    return pl.pallas_call(
        kernel,
        in_specs=[VMEM] * 5,
        out_specs=[VMEM] * 2,
        out_shape=[out, out],
        scratch_shapes=[pltpu.VMEM((3 * depth, 256), BF)],
        compiler_params=params(16),
        cost_estimate=cost(6 * tokens * depth * 256, 6 * tokens * depth + 8 * depth * 256),
        name="forward",
    )(*states, *blocks)


def backward_kernel(other, refs):
    mine, theirs, (s0, s1, s2) = refs[:4], refs[4:8], refs[8:11]
    p2, pm, pp, p0, turned = refs[11:]
    y, xl, z, xh, c, d = place()
    half = (xl + 1) % 2 if other else xl
    for pairs, core in ((mine, c), (theirs, 1 - c)):
        way = 1 - 2 * core
        for ref, zz in zip(pairs, (z, z - way, z + way, z + 2)):
            for j in range(2):
                token = (zz + 4) % 4 * 4 + (xh + j) % 2 * 2 + core
                lanes = pl.ds(pl.multiple_of(token * 128, 128), 128)
                for r, yy in enumerate((y + 2, y - d, y + d, y)):
                    rows = pl.ds(pl.multiple_of(((yy + 4) % 4 * 2 + half) * 128, 128), 128)
                    turned[r * 128:(r + 1) * 128, lanes] = ref[j, rows, :]

    @pl.loop(0, s0.shape[1] // 512)
    def _(i):
        cols = pl.ds(pl.multiple_of(i * 512, 512), 512)
        for s, state in enumerate((s0, s1, s2)):
            product = jnp.dot(turned[...], state[:, cols], preferred_element_type=F32) * (16384 ** -0.5)
            product = product.astype(BF)
            for r, out in enumerate((p2, pm, pp, p0)):
                out[s, :, cols] = product[r * 128:(r + 1) * 128]


def backward(states, masked, other):
    tokens, depth = states[0].shape
    out = jax.ShapeDtypeStruct((3, 128, depth), BF)

    def kernel(*refs):
        backward_kernel(other, refs)

    return pl.pallas_call(
        kernel,
        in_specs=[VMEM] * 11,
        out_specs=[VMEM] * 4,
        out_shape=[out] * 4,
        scratch_shapes=[pltpu.VMEM((512, tokens), BF)],
        compiler_params=params(16),
        cost_estimate=cost(6 * tokens * depth * 512, 6 * tokens * depth + 16 * tokens * 256),
        name="backward_other" if other else "backward_own",
    )(*masked, *states)


def pick_kernel(*refs):
    _, _, z, _, _, d = place()
    count = (len(refs) - 4) // 2
    for out, zz in zip(refs[2 * count:], (z + 2, z - d, z + d, z)):
        k = (zz + 4) % 4
        for i in range(count):
            total = refs[i][k].astype(F32) + refs[count + i][k].astype(F32)
            out[:, :, i * 256:(i + 1) * 256] = total.astype(BF)


def pick(mine, theirs):
    size = sum(a.size for a in mine)
    out = jax.ShapeDtypeStruct((2, 128, 256 * len(mine)), BF)
    return pl.pallas_call(
        pick_kernel,
        out_shape=[out] * 4,
        compiler_params=params(),
        cost_estimate=cost(size, 6 * size),
        name="pick",
    )(*mine, *theirs)


def split_kernel(a0, a1, b, c0, c1, mine, theirs):
    h = lax.axis_index("tp") // 2 % 2
    for out, k in ((mine, h), (theirs, (h + 1) % 2)):
        for i, (a, c) in enumerate(((a0, c0), (a1, c1))):
            total = a[k].astype(F32) + b[i, k].astype(F32) + c[k].astype(F32)
            out[:, i * 512:(i + 1) * 512] = total.astype(BF)


def split(a0, a1, b, c0, c1):
    out = jax.ShapeDtypeStruct((128, 1024), BF)
    return pl.pallas_call(
        split_kernel,
        out_shape=[out] * 2,
        compiler_params=params(),
        cost_estimate=cost(2 * b.size, 8 * b.size),
        name="split",
    )(a0, a1, b, c0, c1)


def pass_kernel(qa, ta, qb, tb, out):
    for i, (q, t) in enumerate(((qa, ta), (qb, tb))):
        out[i] = (q[...].astype(F32) + t[...].astype(F32)).astype(BF)


def pass_on(qa, ta, qb, tb):
    return pl.pallas_call(
        pass_kernel,
        out_shape=jax.ShapeDtypeStruct((2, *qa.shape), BF),
        compiler_params=params(),
        cost_estimate=cost(2 * qa.size, 12 * qa.size),
        name="pass_on",
    )(qa, ta, qb, tb)


def join_kernel(a, b, out):
    y, xl, _, _, _, _ = place()
    spots = (
        (y - 1, xl), (y + 1, xl), (y, xl), (y, xl + 1),
        (y + 2, xl), (y + 2, xl + 1), (y - 1, xl + 1), (y + 1, xl + 1),
    )
    for j, (yy, hh) in enumerate(spots):
        lanes = pl.ds(pl.multiple_of(((yy + 4) % 4 * 2 + hh % 2) * 128, 128), 128)
        cut = slice(j * 128, (j + 1) * 128)
        out[:, lanes] = (a[:, cut].astype(F32) + b[:, cut].astype(F32)).astype(BF)


def join(a, b):
    return pl.pallas_call(
        join_kernel,
        out_shape=jax.ShapeDtypeStruct(a.shape, BF),
        compiler_params=params(),
        cost_estimate=cost(a.size, 6 * a.size),
        name="join",
    )(a, b)


def finish_kernel(a, b, c, e, g0, g1, g2):
    for s, out in enumerate((g0, g1, g2)):
        total = a[s].astype(F32) + b[s].astype(F32) + c[s].astype(F32) + e[s].astype(F32)
        out[...] = total.T.astype(BF)


def finish(a, b, c, e):
    _, cols, depth = a.shape
    return pl.pallas_call(
        finish_kernel,
        out_shape=[jax.ShapeDtypeStruct((depth, cols), BF)] * 3,
        compiler_params=params(),
        cost_estimate=cost(4 * a.size, 10 * a.size),
        name="finish",
    )(a, b, c, e)


def body(low_state, mid_state, high_state, w_low, w_mid, w_high, kv_grad, loss_mask):
    states = (low_state, mid_state, high_state)
    w = collect((w_low, w_mid, w_high))
    a1 = send(w, Y1)
    a2 = send(w, Y2)
    x1 = send(w, XL)

    w, kv_grad = fence(w, kv_grad)
    mt = masked_turned(kv_grad, loss_mask)
    m_h = send(mt, XH)
    mt, *states = fence(mt, *states)
    states = load(*states)

    mt, m_h, *states = fence(mt, m_h, *states)
    pair = jnp.stack((mt, m_h))
    z1 = send(pair, Z1)
    z2 = send(pair, Z2)

    a1, a2, pair, *states = fence(a1, a2, pair, *states)
    a3 = send(a1, Y1)
    pair_o = send(pair, CORE)
    mine_a, theirs_a = forward(states, (a1, a2), True)

    x1, z1, z2, pair_o, mine_a, theirs_a = fence(x1, z1, z2, pair_o, mine_a, theirs_a)
    z3 = send(z1, Z1)
    z1_o = send(z1, CORE)
    b1 = send(x1, Y1)
    b2 = send(x1, Y2)
    b3 = send(a3, XL)
    mine_b, theirs_b = forward(states, (w, x1), False)

    z3, z1_o, z2, mine_b, theirs_b = fence(z3, z1_o, z2, mine_b, theirs_b)
    z2_o = send(z2, CORE)
    z3_o = send(z3, CORE)
    masked = [pair, z1, z2, z3, pair_o, z1_o, z2_o, z3_o]
    p2x, pmx, ppx, p0x = backward(states, masked, True)

    b1, b2, b3, p2x, pmx, ppx, p0x, pair, theirs_a, theirs_b = fence(
        b1, b2, b3, p2x, pmx, ppx, p0x, pair, theirs_a, theirs_b
    )
    e1 = send(p2x, XL)
    e2 = send(pmx, Y2)
    e3 = send(ppx, Y1)
    got_a = send(theirs_a, CORE)
    got_b = send(theirs_b, CORE)
    mine_c, theirs_c = forward(states, (a3, b3), False)
    mine_d, theirs_d = forward(states, (b1, b2), True)
    got_a, got_b, theirs_c, theirs_d, pair = fence(got_a, got_b, theirs_c, theirs_d, pair)
    q2a, qma, qpa, q0a = pick((mine_a, mine_b), (got_a, got_b))
    t3a = send(q2a, Z2)
    t2a = send(qpa, Z1)
    masked = [pair, *masked[1:]]
    p2, pm, pp, p0 = backward(states, masked, False)

    e1, e2, e3, t3a, t2a, theirs_c, theirs_d, p2, pm, pp, p0 = fence(
        e1, e2, e3, t3a, t2a, theirs_c, theirs_d, p2, pm, pp, p0
    )
    f3 = send(add(p2, e1), Y2)
    fx = send(add(p0x, e2, e3), XL)
    got_c = send(theirs_c, CORE)
    got_d = send(theirs_d, CORE)
    q2b, qmb, qpb, q0b = pick((mine_c, mine_d), (got_c, got_d))
    t3b = send(q2b, Z2)
    t2b = send(qpb, Z1)

    t3b, t2b, pm, pp = fence(t3b, t2b, pm, pp)
    t1 = send(pass_on(qma, t3a, qmb, t3b), Z2)
    f1 = send(add(pm, f3), Y2)
    f2 = send(pp, Y1)
    kept, given = split(q0a, q0b, t1, t2a, t2b)
    got, *grads = fence(send(given, XH), *finish(p0, fx, f1, f2))
    return (join(kept, got), *grads)


def solution(mesh):
    in_specs = (
        P("grp", "tp"),
        P("grp", "tp"),
        P("grp", "tp"),
        P("tp", "grp"),
        P("tp", "grp"),
        P("tp", "grp"),
        P(("grp", "tp"), None),
        P(("grp", "tp")),
    )
    out_specs = (P(("grp", "tp"), None), P("tp", "grp"), P("tp", "grp"), P("tp", "grp"))
    return jax.shard_map(body, mesh=mesh, in_specs=in_specs, out_specs=out_specs, check_vma=False)
```

```python
import jax
import jax.numpy as jnp
from jax import lax
from jax.experimental import pallas as pl
from jax.experimental.pallas import tpu as pltpu
from jax.sharding import PartitionSpec as P

BF = jnp.bfloat16
F32 = jnp.float32
MIB = 1024 * 1024
LOAD_MIB = 38
GRP, TP = 8, 16
CHEAP = 1000
FULL = ("grp", "tp")


def full_perm(move):
    pairs = []
    for g in range(GRP):
        for t in range(TP):
            y, xl, z, xh, c = move(g // 2, g % 2, t // 4, t // 2 % 2, t % 2)
            pairs.append((g * TP + t, (y % 4 * 2 + xl % 2) * TP + z % 4 * 4 + xh % 2 * 2 + c % 2))
    return pairs


Y1 = full_perm(lambda y, xl, z, xh, c: (y + 1 - 2 * c, xl, z, xh, c))
Y2 = full_perm(lambda y, xl, z, xh, c: (y - 1 + 2 * c, xl, z, xh, c))
Z1 = full_perm(lambda y, xl, z, xh, c: (y, xl, z + 1 - 2 * c, xh, c))
Z2 = full_perm(lambda y, xl, z, xh, c: (y, xl, z - 1 + 2 * c, xh, c))
XL = full_perm(lambda y, xl, z, xh, c: (y, xl + 1, z, xh, c))
XH = full_perm(lambda y, xl, z, xh, c: (y, xl, z, xh + 1, c))
CORE = full_perm(lambda y, xl, z, xh, c: (y, xl, z, xh, c + 1))


def send(array, pairs):
    return lax.ppermute(array, FULL, pairs)


def add(*arrays):
    total = arrays[0].astype(F32)
    for array in arrays[1:]:
        total = total + array.astype(F32)
    return total.astype(BF)


def place():
    g = lax.axis_index("grp")
    t = lax.axis_index("tp")
    c = t % 2
    return g // 2, g % 2, t // 4, t // 2 % 2, c, 1 - 2 * c


def params(mib=8):
    return pltpu.CompilerParams(vmem_limit_bytes=mib * MIB)


def cost(flops, bytes_accessed):
    return pl.CostEstimate(flops=flops // CHEAP, bytes_accessed=bytes_accessed // CHEAP, transcendentals=0)


def fence(*arrays):
    return lax.optimization_barrier(arrays)


VMEM = pl.BlockSpec(memory_space=pltpu.VMEM)


def prepare_kernel(w0, w1, w2, grad_ref, mask_ref, w_ref, turned_ref, grad, mask, sems):
    depth = w0.shape[0]
    moves = [
        pltpu.make_async_copy(mask_ref, mask, sems.at[0]),
        pltpu.make_async_copy(grad_ref, grad, sems.at[1]),
    ]
    for i, w in enumerate((w0, w1, w2)):
        moves.append(pltpu.make_async_copy(w, w_ref.at[pl.ds(i * depth, depth), :], sems.at[2 + i]))
    for move in moves:
        move.start()
    moves[0].wait()
    moves[1].wait()
    turned_ref[...] = (grad[...].astype(F32).T * mask[...].astype(F32)).astype(BF)
    for move in moves[2:]:
        move.wait()


def prepare(weights, kv_grad, loss_mask):
    rows, cols = kv_grad.shape
    depth, width = weights[0].shape
    return pl.pallas_call(
        prepare_kernel,
        in_specs=[pl.BlockSpec(memory_space=pl.ANY)] * 5,
        out_specs=[VMEM] * 2,
        out_shape=[jax.ShapeDtypeStruct((3 * depth, width), BF), jax.ShapeDtypeStruct((cols, rows), BF)],
        scratch_shapes=[
            pltpu.VMEM((rows, cols), BF),
            pltpu.VMEM((1, rows), jnp.int32),
            pltpu.SemaphoreType.DMA((5,)),
        ],
        compiler_params=params(60),
        cost_estimate=cost(rows * cols, 4 * rows * cols + 12 * depth * width),
        name="prepare",
    )(*weights, kv_grad, loss_mask.reshape(1, rows))


def load_kernel(*refs):
    half = len(refs) // 2
    sems = refs[-1]
    moves = [pltpu.make_async_copy(refs[i], refs[half + i], sems.at[i]) for i in range(half)]
    for move in moves:
        move.start()
    for move in moves:
        move.wait()


def load(*arrays):
    count = len(arrays)
    return pl.pallas_call(
        load_kernel,
        in_specs=[pl.BlockSpec(memory_space=pl.ANY)] * count,
        out_specs=[VMEM] * count,
        out_shape=[jax.ShapeDtypeStruct(a.shape, BF) for a in arrays],
        scratch_shapes=[pltpu.SemaphoreType.DMA((count,))],
        compiler_params=params(LOAD_MIB),
        cost_estimate=cost(0, 4 * sum(a.size for a in arrays)),
        name="load",
    )(*arrays)


def forward_kernel(swap, s0, s1, s2, wa, wb, mine_ref, theirs_ref, w_all):
    c = lax.axis_index("tp") % 2
    for i, w in ((c, wa), (1 - c, wb)) if swap else ((0, wa), (1, wb)):
        w_all[:, pl.ds(pl.multiple_of(i * 128, 128), 128)] = w[...]
    depth = s0.shape[1]
    total = jnp.dot(s0[...], w_all[0:depth, :], preferred_element_type=F32)
    total += jnp.dot(s1[...], w_all[depth:2 * depth, :], preferred_element_type=F32)
    total += jnp.dot(s2[...], w_all[2 * depth:3 * depth, :], preferred_element_type=F32)
    total = total.astype(BF)
    for z in range(4):
        for h in range(2):
            at = (z * 2 + h) * 256
            first = total[at:at + 128]
            second = total[at + 128:at + 256]
            mine_ref[z, h] = jnp.where(c == 0, first, second)
            theirs_ref[z, h] = jnp.where(c == 0, second, first)


def forward(states, blocks, swap):
    tokens, depth = states[0].shape
    out = jax.ShapeDtypeStruct((4, 2, 128, 256), BF)

    def kernel(*refs):
        forward_kernel(swap, *refs)

    return pl.pallas_call(
        kernel,
        in_specs=[VMEM] * 5,
        out_specs=[VMEM] * 2,
        out_shape=[out, out],
        scratch_shapes=[pltpu.VMEM((3 * depth, 256), BF)],
        compiler_params=params(16),
        cost_estimate=cost(6 * tokens * depth * 256, 6 * tokens * depth + 8 * depth * 256),
        name="forward",
    )(*states, *blocks)


def backward_kernel(other, dests, refs):
    near, far, near_o, far_o, s0, s1, s2 = refs[:7]
    outs, turned = refs[7:-1], refs[-1]
    y, xl, z, xh, c, d = place()
    half = (xl + 1) % 2 if other else xl
    spots = {"far": y + 2, "back": y - d, "ahead": y + d, "here": y}
    for ref, core, first in ((near, c, 0), (far, c, 2), (near_o, 1 - c, 0), (far_o, 1 - c, 2)):
        way = 1 - 2 * core
        for j in range(4):
            zz = (z, z - way, z + way, z + 2)[first + j // 2]
            token = (zz + 4) % 4 * 4 + (xh + j % 2) % 2 * 2 + core
            lanes = pl.ds(pl.multiple_of(token * 128, 128), 128)
            for r, dest in enumerate(dests):
                rows = pl.ds(pl.multiple_of(((spots[dest] + 4) % 4 * 2 + half) * 128, 128), 128)
                turned[r * 128:(r + 1) * 128, lanes] = ref[j, rows, :]

    @pl.loop(0, s0.shape[1] // 512)
    def _(i):
        cols = pl.ds(pl.multiple_of(i * 512, 512), 512)
        for s, state in enumerate((s0, s1, s2)):
            product = jnp.dot(turned[...], state[:, cols], preferred_element_type=F32) * (16384 ** -0.5)
            product = product.astype(BF)
            for r, out in enumerate(outs):
                out[s, :, cols] = product[r * 128:(r + 1) * 128]


def backward(states, masked, other, dests):
    tokens, depth = states[0].shape
    count = len(dests)
    out = jax.ShapeDtypeStruct((3, 128, depth), BF)

    def kernel(*refs):
        backward_kernel(other, dests, refs)

    return pl.pallas_call(
        kernel,
        in_specs=[VMEM] * 7,
        out_specs=[VMEM] * count,
        out_shape=[out] * count,
        scratch_shapes=[pltpu.VMEM((128 * count, tokens), BF)],
        compiler_params=params(16),
        cost_estimate=cost(6 * tokens * depth * 128 * count, 6 * tokens * depth + 16 * tokens * 256),
        name="backward",
    )(*masked, *states)


def pick_kernel(*refs):
    _, _, z, _, _, d = place()
    count = (len(refs) - 4) // 2
    for out, zz in zip(refs[2 * count:], (z + 2, z - d, z + d, z)):
        k = (zz + 4) % 4
        for i in range(count):
            total = refs[i][k].astype(F32) + refs[count + i][k].astype(F32)
            out[:, :, i * 256:(i + 1) * 256] = total.astype(BF)


def pick(mine, theirs):
    size = sum(a.size for a in mine)
    out = jax.ShapeDtypeStruct((2, 128, 256 * len(mine)), BF)
    return pl.pallas_call(
        pick_kernel,
        out_shape=[out] * 4,
        compiler_params=params(),
        cost_estimate=cost(size, 6 * size),
        name="pick",
    )(*mine, *theirs)


def split_kernel(a0, a1, b0, b1, c0, c1, mine, theirs):
    h = lax.axis_index("tp") // 2 % 2
    for out, k in ((mine, h), (theirs, (h + 1) % 2)):
        for i, (a, b, c) in enumerate(((a0, b0, c0), (a1, b1, c1))):
            total = a[k].astype(F32) + b[k].astype(F32) + c[k].astype(F32)
            out[:, i * 512:(i + 1) * 512] = total.astype(BF)


def split(a0, a1, b0, b1, c0, c1):
    out = jax.ShapeDtypeStruct((128, 1024), BF)
    return pl.pallas_call(
        split_kernel,
        out_shape=[out] * 2,
        compiler_params=params(),
        cost_estimate=cost(4 * b0.size, 16 * b0.size),
        name="split",
    )(a0, a1, b0, b1, c0, c1)


def join_kernel(a, b, out):
    y, xl, _, _, _, _ = place()
    spots = (
        (y - 1, xl), (y + 1, xl), (y, xl), (y, xl + 1),
        (y + 2, xl), (y + 2, xl + 1), (y - 1, xl + 1), (y + 1, xl + 1),
    )
    for j, (yy, hh) in enumerate(spots):
        lanes = pl.ds(pl.multiple_of(((yy + 4) % 4 * 2 + hh % 2) * 128, 128), 128)
        cut = slice(j * 128, (j + 1) * 128)
        out[:, lanes] = (a[:, cut].astype(F32) + b[:, cut].astype(F32)).astype(BF)


def join(a, b):
    return pl.pallas_call(
        join_kernel,
        out_shape=jax.ShapeDtypeStruct(a.shape, BF),
        compiler_params=params(),
        cost_estimate=cost(a.size, 6 * a.size),
        name="join",
    )(a, b)


def finish_kernel(a, b, c, e, g0, g1, g2):
    for s, out in enumerate((g0, g1, g2)):
        total = a[s].astype(F32) + b[s].astype(F32) + c[s].astype(F32) + e[s].astype(F32)
        out[...] = total.T.astype(BF)


def finish(a, b, c, e):
    _, cols, depth = a.shape
    return pl.pallas_call(
        finish_kernel,
        out_shape=[jax.ShapeDtypeStruct((depth, cols), BF)] * 3,
        compiler_params=params(),
        cost_estimate=cost(4 * a.size, 10 * a.size),
        name="finish",
    )(a, b, c, e)


def body(low_state, mid_state, high_state, w_low, w_mid, w_high, kv_grad, loss_mask):
    states = (low_state, mid_state, high_state)
    w, mt = prepare((w_low, w_mid, w_high), kv_grad, loss_mask)
    a1 = send(w, Y1)
    a2 = send(w, Y2)
    m_h = send(mt, XH)
    m_1 = send(mt, Z1)
    mt, *states = fence(mt, *states)
    states = load(*states)

    mt, m_h, m_1, w, *states = fence(mt, m_h, m_1, w, *states)
    x1 = send(w, XL)
    h_1 = send(m_h, Z1)
    pair = jnp.stack((mt, m_h))
    z2 = send(pair, Z2)

    a1, a2, h_1, *states = fence(a1, a2, h_1, *states)
    a3 = send(a1, Y1)
    z1 = jnp.stack((m_1, h_1))
    z3 = send(z1, Z1)
    mine_a, theirs_a = forward(states, (a1, a2), True)

    x1, z2, z3, mine_a, theirs_a = fence(x1, z2, z3, mine_a, theirs_a)
    near = jnp.concatenate((pair, z1))
    far = jnp.concatenate((z2, z3))
    near_o = send(near, CORE)
    far_o = send(far, CORE)
    b1 = send(x1, Y1)
    b2 = send(x1, Y2)
    b3 = send(a3, XL)
    mine_b, theirs_b = forward(states, (w, x1), False)
    near_o, far_o, mine_b = fence(near_o, far_o, mine_b)
    p2x, pmx, ppx, p0x = backward(states, (near, far, near_o, far_o), True, ("far", "back", "ahead", "here"))
    p0x, near = fence(p0x, near)
    p2, pp = backward(states, (near, far, near_o, far_o), False, ("far", "ahead"))

    b1, b2, p2, pp, p2x, pmx, ppx, p0x, near, theirs_a, theirs_b = fence(
        b1, b2, p2, pp, p2x, pmx, ppx, p0x, near, theirs_a, theirs_b
    )
    e2 = send(pmx, Y2)
    e3 = send(ppx, Y1)
    e1 = send(p2x, XL)
    got_a = send(theirs_a, CORE)
    got_b = send(theirs_b, CORE)
    mine_c, theirs_c = forward(states, (a3, b3), False)
    mine_d, theirs_d = forward(states, (b1, b2), True)
    got_a, got_b, theirs_c, theirs_d, near = fence(got_a, got_b, theirs_c, theirs_d, near)
    q2a, qma, qpa, q0a = pick((mine_a, mine_b), (got_a, got_b))
    t3a = send(q2a, Z2)
    t2a = send(qpa, Z1)
    pm, p0 = backward(states, (near, far, near_o, far_o), False, ("back", "here"))

    e1, e2, e3, t3a, t2a, theirs_c, theirs_d, p2, pm, pp, p0 = fence(
        e1, e2, e3, t3a, t2a, theirs_c, theirs_d, p2, pm, pp, p0
    )
    f3 = send(add(p2, e1), Y2)
    f2 = send(pp, Y1)
    fx = send(add(p0x, e2, e3), XL)
    got_c = send(theirs_c, CORE)
    got_d = send(theirs_d, CORE)
    q2b, qmb, qpb, q0b = pick((mine_c, mine_d), (got_c, got_d))
    t3b = send(q2b, Z2)
    t2b = send(qpb, Z1)

    t3b, t2b, qma, qmb = fence(t3b, t2b, qma, qmb)
    t1a = send(add(qma, t3a), Z2)
    t1b = send(add(qmb, t3b), Z2)
    f1 = send(add(pm, f3), Y2)
    kept, given = split(q0a, q0b, t1a, t1b, t2a, t2b)
    keys_values = join(kept, send(given, XH))
    return (keys_values, *finish(p0, fx, f1, f2))


def solution(mesh):
    in_specs = (
        P("grp", "tp"),
        P("grp", "tp"),
        P("grp", "tp"),
        P("tp", "grp"),
        P("tp", "grp"),
        P("tp", "grp"),
        P(("grp", "tp"), None),
        P(("grp", "tp")),
    )
    out_specs = (P(("grp", "tp"), None), P("tp", "grp"), P("tp", "grp"), P("tp", "grp"))
    return jax.shard_map(body, mesh=mesh, in_specs=in_specs, out_specs=out_specs, check_vma=False)
```

```python
import jax
import jax.numpy as jnp
from jax import lax
from jax.experimental import pallas as pl
from jax.experimental.pallas import tpu as pltpu
from jax.sharding import PartitionSpec as P

BF = jnp.bfloat16
F32 = jnp.float32
MIB = 1024 * 1024
LOAD_MIB = 38
GRP, TP = 8, 16
CHEAP = 1000
FULL = ("grp", "tp")


def full_perm(move):
    pairs = []
    for g in range(GRP):
        for t in range(TP):
            y, xl, z, xh, c = move(g // 2, g % 2, t // 4, t // 2 % 2, t % 2)
            pairs.append((g * TP + t, (y % 4 * 2 + xl % 2) * TP + z % 4 * 4 + xh % 2 * 2 + c % 2))
    return pairs


Y1 = full_perm(lambda y, xl, z, xh, c: (y + 1 - 2 * c, xl, z, xh, c))
Y2 = full_perm(lambda y, xl, z, xh, c: (y - 1 + 2 * c, xl, z, xh, c))
Z1 = full_perm(lambda y, xl, z, xh, c: (y, xl, z + 1 - 2 * c, xh, c))
Z2 = full_perm(lambda y, xl, z, xh, c: (y, xl, z - 1 + 2 * c, xh, c))
XL = full_perm(lambda y, xl, z, xh, c: (y, xl + 1, z, xh, c))
XH = full_perm(lambda y, xl, z, xh, c: (y, xl, z, xh + 1, c))
CORE = full_perm(lambda y, xl, z, xh, c: (y, xl, z, xh, c + 1))


def send(array, pairs):
    return lax.ppermute(array, FULL, pairs)


def add(*arrays):
    total = arrays[0].astype(F32)
    for array in arrays[1:]:
        total = total + array.astype(F32)
    return total.astype(BF)


def place():
    g = lax.axis_index("grp")
    t = lax.axis_index("tp")
    c = t % 2
    return g // 2, g % 2, t // 4, t // 2 % 2, c, 1 - 2 * c


def params(mib=8):
    return pltpu.CompilerParams(vmem_limit_bytes=mib * MIB)


def cost(flops, bytes_accessed):
    return pl.CostEstimate(flops=flops // CHEAP, bytes_accessed=bytes_accessed // CHEAP, transcendentals=0)


def fence(*arrays):
    return lax.optimization_barrier(arrays)


VMEM = pl.BlockSpec(memory_space=pltpu.VMEM)


def prepare_kernel(w0, w1, w2, grad_ref, mask_ref, w_ref, turned_ref, grad, mask, sems):
    depth = w0.shape[0]
    moves = [
        pltpu.make_async_copy(mask_ref, mask, sems.at[0]),
        pltpu.make_async_copy(grad_ref, grad, sems.at[1]),
    ]
    for i, w in enumerate((w0, w1, w2)):
        moves.append(pltpu.make_async_copy(w, w_ref.at[pl.ds(i * depth, depth), :], sems.at[2 + i]))
    for move in moves:
        move.start()
    moves[0].wait()
    moves[1].wait()
    turned_ref[...] = (grad[...].astype(F32).T * mask[...].astype(F32)).astype(BF)
    for move in moves[2:]:
        move.wait()


def prepare(weights, kv_grad, loss_mask):
    rows, cols = kv_grad.shape
    depth, width = weights[0].shape
    return pl.pallas_call(
        prepare_kernel,
        in_specs=[pl.BlockSpec(memory_space=pl.ANY)] * 5,
        out_specs=[VMEM] * 2,
        out_shape=[jax.ShapeDtypeStruct((3 * depth, width), BF), jax.ShapeDtypeStruct((cols, rows), BF)],
        scratch_shapes=[
            pltpu.VMEM((rows, cols), BF),
            pltpu.VMEM((1, rows), jnp.int32),
            pltpu.SemaphoreType.DMA((5,)),
        ],
        compiler_params=params(60),
        cost_estimate=cost(rows * cols, 4 * rows * cols + 12 * depth * width),
        name="prepare",
    )(*weights, kv_grad, loss_mask.reshape(1, rows))


def load_kernel(*refs):
    half = len(refs) // 2
    sems = refs[-1]
    moves = [pltpu.make_async_copy(refs[i], refs[half + i], sems.at[i]) for i in range(half)]
    for move in moves:
        move.start()
    for move in moves:
        move.wait()


def load(*arrays):
    count = len(arrays)
    return pl.pallas_call(
        load_kernel,
        in_specs=[pl.BlockSpec(memory_space=pl.ANY)] * count,
        out_specs=[VMEM] * count,
        out_shape=[jax.ShapeDtypeStruct(a.shape, BF) for a in arrays],
        scratch_shapes=[pltpu.SemaphoreType.DMA((count,))],
        compiler_params=params(LOAD_MIB),
        cost_estimate=cost(0, 4 * sum(a.size for a in arrays)),
        name="load",
    )(*arrays)


def forward_kernel(s0, s1, s2, wa, wb, mine_ref, theirs_ref, w_all):
    c = lax.axis_index("tp") % 2
    w_all[:, 0:128] = wa[...]
    w_all[:, 128:256] = wb[...]
    depth = s0.shape[1]
    total = jnp.dot(s0[...], w_all[0:depth, :], preferred_element_type=F32)
    total += jnp.dot(s1[...], w_all[depth:2 * depth, :], preferred_element_type=F32)
    total += jnp.dot(s2[...], w_all[2 * depth:3 * depth, :], preferred_element_type=F32)
    total = total.astype(BF)
    for z in range(4):
        for h in range(2):
            at = (z * 2 + h) * 256
            first = total[at:at + 128]
            second = total[at + 128:at + 256]
            mine_ref[z, h] = jnp.where(c == 0, first, second)
            theirs_ref[z, h] = jnp.where(c == 0, second, first)


def forward(states, blocks):
    tokens, depth = states[0].shape
    out = jax.ShapeDtypeStruct((4, 2, 128, 256), BF)

    return pl.pallas_call(
        forward_kernel,
        in_specs=[VMEM] * 5,
        out_specs=[VMEM] * 2,
        out_shape=[out, out],
        scratch_shapes=[pltpu.VMEM((3 * depth, 256), BF)],
        compiler_params=params(16),
        cost_estimate=cost(6 * tokens * depth * 256, 6 * tokens * depth + 8 * depth * 256),
        name="forward",
    )(*states, *blocks)


def backward_kernel(other, dests, refs):
    mine, theirs, (s0, s1, s2) = refs[:3], refs[3:6], refs[6:9]
    outs, turned = refs[9:-1], refs[-1]
    y, xl, z, xh, c, d = place()
    half = (xl + 1) % 2 if other else xl
    spots = {"far": y + 2, "back": y - d, "ahead": y + d, "here": y}
    for pieces, core in ((mine, c), (theirs, 1 - c)):
        way = 1 - 2 * core
        beside = ((z - way, xh), (z + way, xh))
        middle = ((z, xh), (z, xh + 1), (z - way, xh + 1), (z + way, xh + 1))
        across = ((z + 2, xh), (z + 2, xh + 1))
        for ref, j, (zz, hh) in (
            (ref, j, at) for ref, ats in zip(pieces, (beside, middle, across)) for j, at in enumerate(ats)
        ):
            token = (zz + 4) % 4 * 4 + hh % 2 * 2 + core
            lanes = pl.ds(pl.multiple_of(token * 128, 128), 128)
            for r, dest in enumerate(dests):
                rows = pl.ds(pl.multiple_of(((spots[dest] + 4) % 4 * 2 + half) * 128, 128), 128)
                turned[r * 128:(r + 1) * 128, lanes] = ref[j, rows, :]

    @pl.loop(0, s0.shape[1] // 512)
    def _(i):
        cols = pl.ds(pl.multiple_of(i * 512, 512), 512)
        for s, state in enumerate((s0, s1, s2)):
            product = jnp.dot(turned[...], state[:, cols], preferred_element_type=F32) * (16384 ** -0.5)
            product = product.astype(BF)
            for r, out in enumerate(outs):
                out[s, :, cols] = product[r * 128:(r + 1) * 128]


def backward(states, masked, other, dests):
    tokens, depth = states[0].shape
    count = len(dests)
    out = jax.ShapeDtypeStruct((3, 128, depth), BF)

    def kernel(*refs):
        backward_kernel(other, dests, refs)

    return pl.pallas_call(
        kernel,
        in_specs=[VMEM] * 9,
        out_specs=[VMEM] * count,
        out_shape=[out] * count,
        scratch_shapes=[pltpu.VMEM((128 * count, tokens), BF)],
        compiler_params=params(16),
        cost_estimate=cost(6 * tokens * depth * 128 * count, 6 * tokens * depth + 16 * tokens * 256),
        name="backward",
    )(*masked, *states)


def pick_kernel(sums, refs):
    _, _, z, _, _, d = place()
    count = (len(refs) - 4) // 2
    mine, theirs = refs[:count], refs[count:2 * count]
    for out, zz in zip(refs[2 * count:], (z + 2, z - d, z + d, z)):
        k = (zz + 4) % 4
        for i, (m, m_half, t, t_half) in enumerate(sums):
            m_cut = slice(m_half * 128, m_half * 128 + 128)
            t_cut = slice(t_half * 128, t_half * 128 + 128)
            total = mine[m][k, :, :, m_cut].astype(F32) + theirs[t][k, :, :, t_cut].astype(F32)
            out[:, :, i * 128:(i + 1) * 128] = total.astype(BF)


def pick(sums, mine, theirs):
    size = sum(a.size for a in mine)
    out = jax.ShapeDtypeStruct((2, 128, 128 * len(sums)), BF)

    def kernel(*refs):
        pick_kernel(sums, refs)

    return pl.pallas_call(
        kernel,
        out_shape=[out] * 4,
        compiler_params=params(),
        cost_estimate=cost(size, 6 * size),
        name="pick",
    )(*mine, *theirs)


def split_kernel(a0, a1, b, c0, c1, mine, theirs):
    h = lax.axis_index("tp") // 2 % 2
    for out, k in ((mine, h), (theirs, (h + 1) % 2)):
        at = 0
        for a, c in ((a0, c0), (a1, c1)):
            cut = slice(at, at + a.shape[2])
            at += a.shape[2]
            out[:, cut] = (a[k].astype(F32) + b[k, :, cut].astype(F32) + c[k].astype(F32)).astype(BF)


def split(a0, a1, b, c0, c1):
    out = jax.ShapeDtypeStruct(b.shape[1:], BF)
    return pl.pallas_call(
        split_kernel,
        out_shape=[out] * 2,
        compiler_params=params(),
        cost_estimate=cost(2 * b.size, 8 * b.size),
        name="split",
    )(a0, a1, b, c0, c1)


def pass_kernel(qa, ta, qb, tb, out):
    at = 0
    for q, t in ((qa, ta), (qb, tb)):
        out[:, :, at:at + q.shape[2]] = (q[...].astype(F32) + t[...].astype(F32)).astype(BF)
        at += q.shape[2]


def pass_on(qa, ta, qb, tb):
    cols = qa.shape[2] + qb.shape[2]
    return pl.pallas_call(
        pass_kernel,
        out_shape=jax.ShapeDtypeStruct((*qa.shape[:2], cols), BF),
        compiler_params=params(),
        cost_estimate=cost(256 * cols, 1536 * cols),
        name="pass_on",
    )(qa, ta, qb, tb)


def join_kernel(a, b, out):
    y, xl, _, _, _, d = place()
    spots = (
        (y, xl), (y, xl + 1), (y + 2, xl),
        (y - d, xl), (y + d, xl), (y - d, xl + 1), (y + 2, xl + 1), (y + d, xl + 1),
    )
    for j, (yy, hh) in enumerate(spots):
        lanes = pl.ds(pl.multiple_of(((yy + 4) % 4 * 2 + hh % 2) * 128, 128), 128)
        cut = slice(j * 128, (j + 1) * 128)
        out[:, lanes] = (a[:, cut].astype(F32) + b[:, cut].astype(F32)).astype(BF)


def join(a, b):
    return pl.pallas_call(
        join_kernel,
        out_shape=jax.ShapeDtypeStruct(a.shape, BF),
        compiler_params=params(),
        cost_estimate=cost(a.size, 6 * a.size),
        name="join",
    )(a, b)


def finish_kernel(a, b, c, e, g0, g1, g2):
    for s, out in enumerate((g0, g1, g2)):
        total = a[s].astype(F32) + b[s].astype(F32) + c[s].astype(F32) + e[s].astype(F32)
        out[...] = total.T.astype(BF)


def finish(a, b, c, e):
    _, cols, depth = a.shape
    return pl.pallas_call(
        finish_kernel,
        out_shape=[jax.ShapeDtypeStruct((depth, cols), BF)] * 3,
        compiler_params=params(),
        cost_estimate=cost(4 * a.size, 10 * a.size),
        name="finish",
    )(a, b, c, e)


def body(low_state, mid_state, high_state, w_low, w_mid, w_high, kv_grad, loss_mask):
    states = (low_state, mid_state, high_state)
    w, mt = prepare((w_low, w_mid, w_high), kv_grad, loss_mask)
    a1 = send(w, Y1)
    x1 = send(w, XL)
    m_h = send(mt, XH)
    m_1 = send(mt, Z1)
    m_2 = send(mt, Z2)
    mt, *states = fence(mt, *states)
    states = load(*states)

    a1, mt, m_h, m_1, m_2, w, *states = fence(a1, mt, m_h, m_1, m_2, w, *states)
    a3 = send(a1, Y1)
    h_1 = send(m_h, Z1)
    h_2 = send(m_h, Z2)
    beside = jnp.stack((m_1, m_2))
    beside_o = send(beside, CORE)

    mine_a, theirs_a = forward(states, (w, a1))

    a3, x1, h_1, h_2, beside_o, w, theirs_a, *states = fence(a3, x1, h_1, h_2, beside_o, w, theirs_a, *states)
    a2 = send(w, Y2)
    b1 = send(x1, Y1)
    b3 = send(a3, XL)
    across = send(jnp.stack((m_1, h_1)), Z1)
    middle = jnp.stack((mt, m_h, h_1, h_2))
    middle_o = send(middle, CORE)
    mine_b, theirs_b = forward(states, (x1, a3))

    across, middle_o, x1, theirs_b = fence(across, middle_o, x1, theirs_b)
    across_o = send(across, CORE)
    b2 = send(x1, Y2)
    masked = (beside, middle, across, beside_o, middle_o, across_o)
    p2x, pmx, ppx, p0x = backward(states, masked, True, ("far", "back", "ahead", "here"))

    a2, b1, b3, p2x, pmx, ppx, p0x, beside = fence(a2, b1, b3, p2x, pmx, ppx, p0x, beside)
    e2 = send(pmx, Y2)
    e3 = send(ppx, Y1)
    e1 = send(p2x, XL)
    got_a = send(theirs_a, CORE)
    got_b = send(theirs_b, CORE)
    p2, pm, pp, p0 = backward(states, masked, False, ("far", "back", "ahead", "here"))

    got_a, got_b, p0, b1, a3 = fence(got_a, got_b, p0, b1, a3)
    sums = ((0, 0, 0, 0), (1, 0, 1, 0), (1, 1, 1, 1))
    q2a, qma, qpa, q0a = pick(sums, (mine_a, mine_b), (got_a, got_b))
    t3a = send(q2a, Z2)
    t2a = send(qpa, Z1)
    qma, b1, b3 = fence(qma, b1, b3)
    mine_c, theirs_c = forward(states, (a2, b1))
    mine_d, theirs_d = forward(states, (b3, b2))

    e1, e2, e3, t3a, t2a, theirs_c, theirs_d, p2, pm, pp, p0 = fence(
        e1, e2, e3, t3a, t2a, theirs_c, theirs_d, p2, pm, pp, p0
    )
    got_c = send(theirs_c, CORE)
    got_d = send(theirs_d, CORE)
    f3 = send(add(p2, e1), Y2)
    f2 = send(pp, Y1)
    fx = send(add(p0x, e2, e3), XL)
    sums = ((0, 1, 1, 0), (1, 0, 0, 1), (1, 1, 2, 1), (2, 0, 2, 0), (2, 1, 1, 1))
    q2b, qmb, qpb, q0b = pick(sums, (mine_a, mine_c, mine_d), (got_a, got_c, got_d))
    t3b = send(q2b, Z2)
    t2b = send(qpb, Z1)

    t3b, t2b, qma, qmb = fence(t3b, t2b, qma, qmb)
    t1 = send(pass_on(qma, t3a, qmb, t3b), Z2)
    f1 = send(add(pm, f3), Y2)
    kept, given = split(q0a, q0b, t1, t2a, t2b)
    got, *grads = fence(send(given, XH), *finish(p0, fx, f1, f2))
    return (join(kept, got), *grads)


def solution(mesh):
    in_specs = (
        P("grp", "tp"),
        P("grp", "tp"),
        P("grp", "tp"),
        P("tp", "grp"),
        P("tp", "grp"),
        P("tp", "grp"),
        P(("grp", "tp"), None),
        P(("grp", "tp")),
    )
    out_specs = (P(("grp", "tp"), None), P("tp", "grp"), P("tp", "grp"), P("tp", "grp"))
    return jax.shard_map(body, mesh=mesh, in_specs=in_specs, out_specs=out_specs, check_vma=False)
```

```python
import jax
import jax.numpy as jnp
from jax import lax
from jax.experimental import pallas as pl
from jax.experimental.pallas import tpu as pltpu
from jax.sharding import PartitionSpec as P

BF = jnp.bfloat16
F32 = jnp.float32
MIB = 1024 * 1024
LOAD_MIB = 38
GRP, TP = 8, 16
CHEAP = 1000
FULL = ("grp", "tp")


def full_perm(move):
    pairs = []
    for g in range(GRP):
        for t in range(TP):
            y, xl, z, xh, c = move(g // 2, g % 2, t // 4, t // 2 % 2, t % 2)
            pairs.append((g * TP + t, (y % 4 * 2 + xl % 2) * TP + z % 4 * 4 + xh % 2 * 2 + c % 2))
    return pairs


Y1 = full_perm(lambda y, xl, z, xh, c: (y + 1 - 2 * c, xl, z, xh, c))
Y2 = full_perm(lambda y, xl, z, xh, c: (y - 1 + 2 * c, xl, z, xh, c))
Z1 = full_perm(lambda y, xl, z, xh, c: (y, xl, z + 1 - 2 * c, xh, c))
Z2 = full_perm(lambda y, xl, z, xh, c: (y, xl, z - 1 + 2 * c, xh, c))
XL = full_perm(lambda y, xl, z, xh, c: (y, xl + 1, z, xh, c))
XH = full_perm(lambda y, xl, z, xh, c: (y, xl, z, xh + 1, c))
CORE = full_perm(lambda y, xl, z, xh, c: (y, xl, z, xh, c + 1))


def send(array, pairs):
    return lax.ppermute(array, FULL, pairs)


def add(*arrays):
    total = arrays[0].astype(F32)
    for array in arrays[1:]:
        total = total + array.astype(F32)
    return total.astype(BF)


def place():
    g = lax.axis_index("grp")
    t = lax.axis_index("tp")
    c = t % 2
    return g // 2, g % 2, t // 4, t // 2 % 2, c, 1 - 2 * c


def params(mib=8):
    return pltpu.CompilerParams(vmem_limit_bytes=mib * MIB)


def cost(flops, bytes_accessed):
    return pl.CostEstimate(flops=flops // CHEAP, bytes_accessed=bytes_accessed // CHEAP, transcendentals=0)


def fence(*arrays):
    return lax.optimization_barrier(arrays)


VMEM = pl.BlockSpec(memory_space=pltpu.VMEM)


def prepare_kernel(w0, w1, w2, grad_ref, mask_ref, w_ref, turned_ref, grad, mask, sems):
    depth = w0.shape[0]
    moves = [
        pltpu.make_async_copy(mask_ref, mask, sems.at[0]),
        pltpu.make_async_copy(grad_ref, grad, sems.at[1]),
    ]
    for i, w in enumerate((w0, w1, w2)):
        moves.append(pltpu.make_async_copy(w, w_ref.at[pl.ds(i * depth, depth), :], sems.at[2 + i]))
    for move in moves:
        move.start()
    moves[0].wait()
    moves[1].wait()
    turned_ref[...] = (grad[...].astype(F32).T * mask[...].astype(F32)).astype(BF)
    for move in moves[2:]:
        move.wait()


def prepare(weights, kv_grad, loss_mask):
    rows, cols = kv_grad.shape
    depth, width = weights[0].shape
    return pl.pallas_call(
        prepare_kernel,
        in_specs=[pl.BlockSpec(memory_space=pl.ANY)] * 5,
        out_specs=[VMEM] * 2,
        out_shape=[jax.ShapeDtypeStruct((3 * depth, width), BF), jax.ShapeDtypeStruct((cols, rows), BF)],
        scratch_shapes=[
            pltpu.VMEM((rows, cols), BF),
            pltpu.VMEM((1, rows), jnp.int32),
            pltpu.SemaphoreType.DMA((5,)),
        ],
        compiler_params=params(60),
        cost_estimate=cost(rows * cols, 4 * rows * cols + 12 * depth * width),
        name="prepare",
    )(*weights, kv_grad, loss_mask.reshape(1, rows))


def load_kernel(*refs):
    half = len(refs) // 2
    sems = refs[-1]
    moves = [pltpu.make_async_copy(refs[i], refs[half + i], sems.at[i]) for i in range(half)]
    for move in moves:
        move.start()
    for move in moves:
        move.wait()


def load(*arrays):
    count = len(arrays)
    return pl.pallas_call(
        load_kernel,
        in_specs=[pl.BlockSpec(memory_space=pl.ANY)] * count,
        out_specs=[VMEM] * count,
        out_shape=[jax.ShapeDtypeStruct(a.shape, BF) for a in arrays],
        scratch_shapes=[pltpu.SemaphoreType.DMA((count,))],
        compiler_params=params(LOAD_MIB),
        cost_estimate=cost(0, 4 * sum(a.size for a in arrays)),
        name="load",
    )(*arrays)


def forward_kernel(s0, s1, s2, wa, wb, mine_ref, theirs_ref, w_all):
    c = lax.axis_index("tp") % 2
    w_all[:, 0:128] = wa[...]
    w_all[:, 128:256] = wb[...]
    depth = s0.shape[1]
    total = jnp.dot(s0[...], w_all[0:depth, :], preferred_element_type=F32)
    total += jnp.dot(s1[...], w_all[depth:2 * depth, :], preferred_element_type=F32)
    total += jnp.dot(s2[...], w_all[2 * depth:3 * depth, :], preferred_element_type=F32)
    total = total.astype(BF)
    for z in range(4):
        for h in range(2):
            at = (z * 2 + h) * 256
            first = total[at:at + 128]
            second = total[at + 128:at + 256]
            mine_ref[z, h] = jnp.where(c == 0, first, second)
            theirs_ref[z, h] = jnp.where(c == 0, second, first)


def forward(states, blocks):
    tokens, depth = states[0].shape
    out = jax.ShapeDtypeStruct((4, 2, 128, 256), BF)

    return pl.pallas_call(
        forward_kernel,
        in_specs=[VMEM] * 5,
        out_specs=[VMEM] * 2,
        out_shape=[out, out],
        scratch_shapes=[pltpu.VMEM((3 * depth, 256), BF)],
        compiler_params=params(16),
        cost_estimate=cost(6 * tokens * depth * 256, 6 * tokens * depth + 8 * depth * 256),
        name="forward",
    )(*states, *blocks)


def backward_kernel(other, dests, refs):
    mine, theirs, (s0, s1, s2) = refs[:4], refs[4:8], refs[8:11]
    outs, turned = refs[11:-1], refs[-1]
    y, xl, z, xh, c, d = place()
    half = (xl + 1) % 2 if other else xl
    spots = {"far": y + 2, "back": y - d, "ahead": y + d, "here": y}
    for pieces, core in ((mine, c), (theirs, 1 - c)):
        way = 1 - 2 * core
        pair = ((z, xh), (z, xh + 1))
        back = ((z - way, xh), (z - way, xh + 1))
        ahead = ((z + way, xh), (z + way, xh + 1))
        across = ((z + 2, xh), (z + 2, xh + 1))
        for ref, j, (zz, hh) in (
            (ref, j, at) for ref, ats in zip(pieces, (pair, back, ahead, across)) for j, at in enumerate(ats)
        ):
            token = (zz + 4) % 4 * 4 + hh % 2 * 2 + core
            lanes = pl.ds(pl.multiple_of(token * 128, 128), 128)
            for r, dest in enumerate(dests):
                rows = pl.ds(pl.multiple_of(((spots[dest] + 4) % 4 * 2 + half) * 128, 128), 128)
                turned[r * 128:(r + 1) * 128, lanes] = ref[j, rows, :]

    @pl.loop(0, s0.shape[1] // 512)
    def _(i):
        cols = pl.ds(pl.multiple_of(i * 512, 512), 512)
        for s, state in enumerate((s0, s1, s2)):
            product = jnp.dot(turned[...], state[:, cols], preferred_element_type=F32) * (16384 ** -0.5)
            product = product.astype(BF)
            for r, out in enumerate(outs):
                out[s, :, cols] = product[r * 128:(r + 1) * 128]


def backward(states, masked, other, dests):
    tokens, depth = states[0].shape
    count = len(dests)
    out = jax.ShapeDtypeStruct((3, 128, depth), BF)

    def kernel(*refs):
        backward_kernel(other, dests, refs)

    return pl.pallas_call(
        kernel,
        in_specs=[VMEM] * 11,
        out_specs=[VMEM] * count,
        out_shape=[out] * count,
        scratch_shapes=[pltpu.VMEM((128 * count, tokens), BF)],
        compiler_params=params(16),
        cost_estimate=cost(6 * tokens * depth * 128 * count, 6 * tokens * depth + 16 * tokens * 256),
        name="backward",
    )(*masked, *states)


def pick_kernel(sums, refs):
    _, _, z, _, _, d = place()
    count = (len(refs) - 4) // 2
    mine, theirs = refs[:count], refs[count:2 * count]
    for out, zz in zip(refs[2 * count:], (z + 2, z - d, z + d, z)):
        k = (zz + 4) % 4
        for i, (m, m_half, t, t_half) in enumerate(sums):
            m_cut = slice(m_half * 128, m_half * 128 + 128)
            t_cut = slice(t_half * 128, t_half * 128 + 128)
            total = mine[m][k, :, :, m_cut].astype(F32) + theirs[t][k, :, :, t_cut].astype(F32)
            out[:, :, i * 128:(i + 1) * 128] = total.astype(BF)


def pick(sums, mine, theirs):
    size = sum(a.size for a in mine)
    out = jax.ShapeDtypeStruct((2, 128, 128 * len(sums)), BF)

    def kernel(*refs):
        pick_kernel(sums, refs)

    return pl.pallas_call(
        kernel,
        out_shape=[out] * 4,
        compiler_params=params(),
        cost_estimate=cost(size, 6 * size),
        name="pick",
    )(*mine, *theirs)


def split_kernel(a0, a1, b, c0, c1, mine, theirs):
    h = lax.axis_index("tp") // 2 % 2
    for out, k in ((mine, h), (theirs, (h + 1) % 2)):
        at = 0
        for a, c in ((a0, c0), (a1, c1)):
            cut = slice(at, at + a.shape[2])
            at += a.shape[2]
            out[:, cut] = (a[k].astype(F32) + b[k, :, cut].astype(F32) + c[k].astype(F32)).astype(BF)


def split(a0, a1, b, c0, c1):
    out = jax.ShapeDtypeStruct(b.shape[1:], BF)
    return pl.pallas_call(
        split_kernel,
        out_shape=[out] * 2,
        compiler_params=params(),
        cost_estimate=cost(2 * b.size, 8 * b.size),
        name="split",
    )(a0, a1, b, c0, c1)


def pass_kernel(qa, ta, qb, tb, out):
    at = 0
    for q, t in ((qa, ta), (qb, tb)):
        out[:, :, at:at + q.shape[2]] = (q[...].astype(F32) + t[...].astype(F32)).astype(BF)
        at += q.shape[2]


def pass_on(qa, ta, qb, tb):
    cols = qa.shape[2] + qb.shape[2]
    return pl.pallas_call(
        pass_kernel,
        out_shape=jax.ShapeDtypeStruct((*qa.shape[:2], cols), BF),
        compiler_params=params(),
        cost_estimate=cost(256 * cols, 1536 * cols),
        name="pass_on",
    )(qa, ta, qb, tb)


def join_kernel(a, b, out):
    y, xl, _, _, _, d = place()
    spots = (
        (y, xl), (y, xl + 1), (y + 2, xl),
        (y - d, xl), (y + d, xl), (y - d, xl + 1), (y + 2, xl + 1), (y + d, xl + 1),
    )
    for j, (yy, hh) in enumerate(spots):
        lanes = pl.ds(pl.multiple_of(((yy + 4) % 4 * 2 + hh % 2) * 128, 128), 128)
        cut = slice(j * 128, (j + 1) * 128)
        out[:, lanes] = (a[:, cut].astype(F32) + b[:, cut].astype(F32)).astype(BF)


def join(a, b):
    return pl.pallas_call(
        join_kernel,
        out_shape=jax.ShapeDtypeStruct(a.shape, BF),
        compiler_params=params(),
        cost_estimate=cost(a.size, 6 * a.size),
        name="join",
    )(a, b)


def finish_kernel(a, b, c, e, g0, g1, g2):
    for s, out in enumerate((g0, g1, g2)):
        total = a[s].astype(F32) + b[s].astype(F32) + c[s].astype(F32) + e[s].astype(F32)
        out[...] = total.T.astype(BF)


def finish(a, b, c, e):
    _, cols, depth = a.shape
    return pl.pallas_call(
        finish_kernel,
        out_shape=[jax.ShapeDtypeStruct((depth, cols), BF)] * 3,
        compiler_params=params(),
        cost_estimate=cost(4 * a.size, 10 * a.size),
        name="finish",
    )(a, b, c, e)


def body(low_state, mid_state, high_state, w_low, w_mid, w_high, kv_grad, loss_mask):
    states = (low_state, mid_state, high_state)
    w, mt = prepare((w_low, w_mid, w_high), kv_grad, loss_mask)
    a1 = send(w, Y1)
    a2 = send(w, Y2)
    x1 = send(w, XL)
    m_h = send(mt, XH)
    mt, *states = fence(mt, *states)
    states = load(*states)

    mt, m_h, *states = fence(mt, m_h, *states)
    pair = jnp.stack((mt, m_h))
    z1 = send(pair, Z1)
    z2 = send(pair, Z2)

    a1, a2, w, pair = fence(a1, a2, w, pair)
    a3 = send(a1, Y1)
    pair_o = send(pair, CORE)
    mine_a, theirs_a = forward(states, (w, a1))

    x1, z1, z2, pair_o, theirs_a, *states = fence(x1, z1, z2, pair_o, theirs_a, *states)
    b1 = send(x1, Y1)
    b3 = send(a3, XL)
    across = send(z1, Z1)
    z1_o = send(z1, CORE)
    z2_o = send(z2, CORE)
    mine_b, theirs_b = forward(states, (x1, a3))

    across, z1_o, z2_o, x1, theirs_b = fence(across, z1_o, z2_o, x1, theirs_b)
    across_o = send(across, CORE)
    b2 = send(x1, Y2)
    masked = (pair, z1, z2, across, pair_o, z1_o, z2_o, across_o)
    p2x, pmx, ppx, p0x = backward(states, masked, True, ("far", "back", "ahead", "here"))

    b1, b3, p2x, pmx, ppx, p0x, pair = fence(b1, b3, p2x, pmx, ppx, p0x, pair)
    masked = (pair, *masked[1:])
    e2 = send(pmx, Y2)
    e3 = send(ppx, Y1)
    e1 = send(p2x, XL)
    got_a = send(theirs_a, CORE)
    got_b = send(theirs_b, CORE)
    p2, pm, pp, p0 = backward(states, masked, False, ("far", "back", "ahead", "here"))

    got_a, got_b, p0, b1, a3 = fence(got_a, got_b, p0, b1, a3)
    sums = ((0, 0, 0, 0), (1, 0, 1, 0), (1, 1, 1, 1))
    q2a, qma, qpa, q0a = pick(sums, (mine_a, mine_b), (got_a, got_b))
    t3a = send(q2a, Z2)
    t2a = send(qpa, Z1)
    qma, b1, b3 = fence(qma, b1, b3)
    mine_c, theirs_c = forward(states, (a2, b1))
    mine_d, theirs_d = forward(states, (b3, b2))

    e1, e2, e3, t3a, t2a, theirs_c, theirs_d, p2, pm, pp, p0 = fence(
        e1, e2, e3, t3a, t2a, theirs_c, theirs_d, p2, pm, pp, p0
    )
    got_c = send(theirs_c, CORE)
    got_d = send(theirs_d, CORE)
    f3 = send(add(p2, e1), Y2)
    f2 = send(pp, Y1)
    fx = send(add(p0x, e2, e3), XL)
    sums = ((0, 1, 1, 0), (1, 0, 0, 1), (1, 1, 2, 1), (2, 0, 2, 0), (2, 1, 1, 1))
    q2b, qmb, qpb, q0b = pick(sums, (mine_a, mine_c, mine_d), (got_a, got_c, got_d))
    t3b = send(q2b, Z2)
    t2b = send(qpb, Z1)

    t3b, t2b, qma, qmb = fence(t3b, t2b, qma, qmb)
    t1 = send(pass_on(qma, t3a, qmb, t3b), Z2)
    f1 = send(add(pm, f3), Y2)
    kept, given = split(q0a, q0b, t1, t2a, t2b)
    got, *grads = fence(send(given, XH), *finish(p0, fx, f1, f2))
    return (join(kept, got), *grads)


def solution(mesh):
    in_specs = (
        P("grp", "tp"),
        P("grp", "tp"),
        P("grp", "tp"),
        P("tp", "grp"),
        P("tp", "grp"),
        P("tp", "grp"),
        P(("grp", "tp"), None),
        P(("grp", "tp")),
    )
    out_specs = (P(("grp", "tp"), None), P("tp", "grp"), P("tp", "grp"), P("tp", "grp"))
    return jax.shard_map(body, mesh=mesh, in_specs=in_specs, out_specs=out_specs, check_vma=False)
```

```python
import jax
import jax.numpy as jnp
from jax import lax
from jax.experimental import pallas as pl
from jax.experimental.pallas import tpu as pltpu
from jax.sharding import PartitionSpec as P

BF = jnp.bfloat16
F32 = jnp.float32
MIB = 1024 * 1024
LOAD_MIB = 38
GRP, TP = 8, 16
CHEAP = 1000
FULL = ("grp", "tp")


def full_perm(move):
    pairs = []
    for g in range(GRP):
        for t in range(TP):
            y, xl, z, xh, c = move(g // 2, g % 2, t // 4, t // 2 % 2, t % 2)
            pairs.append((g * TP + t, (y % 4 * 2 + xl % 2) * TP + z % 4 * 4 + xh % 2 * 2 + c % 2))
    return pairs


Y1 = full_perm(lambda y, xl, z, xh, c: (y + 1 - 2 * c, xl, z, xh, c))
Y2 = full_perm(lambda y, xl, z, xh, c: (y - 1 + 2 * c, xl, z, xh, c))
Z1 = full_perm(lambda y, xl, z, xh, c: (y, xl, z + 1 - 2 * c, xh, c))
Z2 = full_perm(lambda y, xl, z, xh, c: (y, xl, z - 1 + 2 * c, xh, c))
XL = full_perm(lambda y, xl, z, xh, c: (y, xl + 1, z, xh, c))
XH = full_perm(lambda y, xl, z, xh, c: (y, xl, z, xh + 1, c))
CORE = full_perm(lambda y, xl, z, xh, c: (y, xl, z, xh, c + 1))


def send(array, pairs):
    return lax.ppermute(array, FULL, pairs)


def add(*arrays):
    total = arrays[0].astype(F32)
    for array in arrays[1:]:
        total = total + array.astype(F32)
    return total.astype(BF)


def place():
    g = lax.axis_index("grp")
    t = lax.axis_index("tp")
    c = t % 2
    return g // 2, g % 2, t // 4, t // 2 % 2, c, 1 - 2 * c


def params(mib=8):
    return pltpu.CompilerParams(vmem_limit_bytes=mib * MIB)


def cost(flops, bytes_accessed):
    return pl.CostEstimate(flops=flops // CHEAP, bytes_accessed=bytes_accessed // CHEAP, transcendentals=0)


def fence(*arrays):
    return lax.optimization_barrier(arrays)


VMEM = pl.BlockSpec(memory_space=pltpu.VMEM)


def prepare_kernel(w0, w1, w2, grad_ref, mask_ref, w_ref, turned_ref, grad, mask, sems):
    depth = w0.shape[0]
    moves = [
        pltpu.make_async_copy(mask_ref, mask, sems.at[0]),
        pltpu.make_async_copy(grad_ref, grad, sems.at[1]),
    ]
    for i, w in enumerate((w0, w1, w2)):
        moves.append(pltpu.make_async_copy(w, w_ref.at[pl.ds(i * depth, depth), :], sems.at[2 + i]))
    for move in moves:
        move.start()
    moves[0].wait()
    moves[1].wait()
    turned_ref[...] = (grad[...].astype(F32).T * mask[...].astype(F32)).astype(BF)
    for move in moves[2:]:
        move.wait()


def prepare(weights, kv_grad, loss_mask):
    rows, cols = kv_grad.shape
    depth, width = weights[0].shape
    return pl.pallas_call(
        prepare_kernel,
        in_specs=[pl.BlockSpec(memory_space=pl.ANY)] * 5,
        out_specs=[VMEM] * 2,
        out_shape=[jax.ShapeDtypeStruct((3 * depth, width), BF), jax.ShapeDtypeStruct((cols, rows), BF)],
        scratch_shapes=[
            pltpu.VMEM((rows, cols), BF),
            pltpu.VMEM((1, rows), jnp.int32),
            pltpu.SemaphoreType.DMA((5,)),
        ],
        compiler_params=params(60),
        cost_estimate=cost(rows * cols, 4 * rows * cols + 12 * depth * width),
        name="prepare",
    )(*weights, kv_grad, loss_mask.reshape(1, rows))


def load_kernel(*refs):
    half = len(refs) // 2
    sems = refs[-1]
    moves = [pltpu.make_async_copy(refs[i], refs[half + i], sems.at[i]) for i in range(half)]
    for move in moves:
        move.start()
    for move in moves:
        move.wait()


def load(*arrays):
    count = len(arrays)
    return pl.pallas_call(
        load_kernel,
        in_specs=[pl.BlockSpec(memory_space=pl.ANY)] * count,
        out_specs=[VMEM] * count,
        out_shape=[jax.ShapeDtypeStruct(a.shape, BF) for a in arrays],
        scratch_shapes=[pltpu.SemaphoreType.DMA((count,))],
        compiler_params=params(LOAD_MIB),
        cost_estimate=cost(0, 4 * sum(a.size for a in arrays)),
        name="load",
    )(*arrays)


def forward_kernel(s0, s1, s2, wa, wb, mine_ref, theirs_ref, w_all):
    c = lax.axis_index("tp") % 2
    w_all[:, 0:128] = wa[...]
    w_all[:, 128:256] = wb[...]
    depth = s0.shape[1]
    total = jnp.dot(s0[...], w_all[0:depth, :], preferred_element_type=F32)
    total += jnp.dot(s1[...], w_all[depth:2 * depth, :], preferred_element_type=F32)
    total += jnp.dot(s2[...], w_all[2 * depth:3 * depth, :], preferred_element_type=F32)
    total = total.astype(BF)
    for z in range(4):
        for h in range(2):
            at = (z * 2 + h) * 256
            first = total[at:at + 128]
            second = total[at + 128:at + 256]
            mine_ref[z, h] = jnp.where(c == 0, first, second)
            theirs_ref[z, h] = jnp.where(c == 0, second, first)


def forward(states, blocks):
    tokens, depth = states[0].shape
    out = jax.ShapeDtypeStruct((4, 2, 128, 256), BF)

    return pl.pallas_call(
        forward_kernel,
        in_specs=[VMEM] * 5,
        out_specs=[VMEM] * 2,
        out_shape=[out, out],
        scratch_shapes=[pltpu.VMEM((3 * depth, 256), BF)],
        compiler_params=params(16),
        cost_estimate=cost(6 * tokens * depth * 256, 6 * tokens * depth + 8 * depth * 256),
        name="forward",
    )(*states, *blocks)


def backward_kernel(other, dests, refs):
    mine, theirs, (s0, s1, s2) = refs[:4], refs[4:8], refs[8:11]
    outs, turned = refs[11:-1], refs[-1]
    y, xl, z, xh, c, d = place()
    half = (xl + 1) % 2 if other else xl
    spots = {"far": y + 2, "back": y - d, "ahead": y + d, "here": y}
    for pieces, core in ((mine, c), (theirs, 1 - c)):
        way = 1 - 2 * core
        pair = ((z, xh), (z, xh + 1))
        back = ((z - way, xh), (z - way, xh + 1))
        ahead = ((z + way, xh), (z + way, xh + 1))
        across = ((z + 2, xh), (z + 2, xh + 1))
        for ref, j, (zz, hh) in (
            (ref, j, at) for ref, ats in zip(pieces, (pair, back, ahead, across)) for j, at in enumerate(ats)
        ):
            token = (zz + 4) % 4 * 4 + hh % 2 * 2 + core
            lanes = pl.ds(pl.multiple_of(token * 128, 128), 128)
            for r, dest in enumerate(dests):
                rows = pl.ds(pl.multiple_of(((spots[dest] + 4) % 4 * 2 + half) * 128, 128), 128)
                turned[r * 128:(r + 1) * 128, lanes] = ref[j, rows, :]

    @pl.loop(0, s0.shape[1] // 512)
    def _(i):
        cols = pl.ds(pl.multiple_of(i * 512, 512), 512)
        for s, state in enumerate((s0, s1, s2)):
            product = jnp.dot(turned[...], state[:, cols], preferred_element_type=F32) * (16384 ** -0.5)
            product = product.astype(BF)
            for r, out in enumerate(outs):
                out[s, :, cols] = product[r * 128:(r + 1) * 128]


def backward(states, masked, other, dests):
    tokens, depth = states[0].shape
    count = len(dests)
    out = jax.ShapeDtypeStruct((3, 128, depth), BF)

    def kernel(*refs):
        backward_kernel(other, dests, refs)

    return pl.pallas_call(
        kernel,
        in_specs=[VMEM] * 11,
        out_specs=[VMEM] * count,
        out_shape=[out] * count,
        scratch_shapes=[pltpu.VMEM((128 * count, tokens), BF)],
        compiler_params=params(16),
        cost_estimate=cost(6 * tokens * depth * 128 * count, 6 * tokens * depth + 16 * tokens * 256),
        name="backward",
    )(*masked, *states)


def pick_kernel(sums, refs):
    _, _, z, _, _, d = place()
    count = (len(refs) - 4) // 2
    mine, theirs = refs[:count], refs[count:2 * count]
    for out, zz in zip(refs[2 * count:], (z + 2, z - d, z + d, z)):
        k = (zz + 4) % 4
        for i, (m, m_half, t, t_half) in enumerate(sums):
            m_cut = slice(m_half * 128, m_half * 128 + 128)
            t_cut = slice(t_half * 128, t_half * 128 + 128)
            total = mine[m][k, :, :, m_cut].astype(F32) + theirs[t][k, :, :, t_cut].astype(F32)
            out[:, :, i * 128:(i + 1) * 128] = total.astype(BF)


def pick(sums, mine, theirs):
    size = sum(a.size for a in mine)
    out = jax.ShapeDtypeStruct((2, 128, 128 * len(sums)), BF)

    def kernel(*refs):
        pick_kernel(sums, refs)

    return pl.pallas_call(
        kernel,
        out_shape=[out] * 4,
        compiler_params=params(),
        cost_estimate=cost(size, 6 * size),
        name="pick",
    )(*mine, *theirs)


def split_kernel(a0, a1, b, c0, c1, mine, theirs):
    h = lax.axis_index("tp") // 2 % 2
    for out, k in ((mine, h), (theirs, (h + 1) % 2)):
        at = 0
        for a, c in ((a0, c0), (a1, c1)):
            cut = slice(at, at + a.shape[2])
            at += a.shape[2]
            out[:, cut] = (a[k].astype(F32) + b[k, :, cut].astype(F32) + c[k].astype(F32)).astype(BF)


def split(a0, a1, b, c0, c1):
    out = jax.ShapeDtypeStruct(b.shape[1:], BF)
    return pl.pallas_call(
        split_kernel,
        out_shape=[out] * 2,
        compiler_params=params(),
        cost_estimate=cost(2 * b.size, 8 * b.size),
        name="split",
    )(a0, a1, b, c0, c1)


def pass_kernel(qa, ta, qb, tb, out):
    at = 0
    for q, t in ((qa, ta), (qb, tb)):
        out[:, :, at:at + q.shape[2]] = (q[...].astype(F32) + t[...].astype(F32)).astype(BF)
        at += q.shape[2]


def pass_on(qa, ta, qb, tb):
    cols = qa.shape[2] + qb.shape[2]
    return pl.pallas_call(
        pass_kernel,
        out_shape=jax.ShapeDtypeStruct((*qa.shape[:2], cols), BF),
        compiler_params=params(),
        cost_estimate=cost(256 * cols, 1536 * cols),
        name="pass_on",
    )(qa, ta, qb, tb)


def join_kernel(a, b, out):
    y, xl, _, _, _, d = place()
    spots = (
        (y, xl), (y, xl + 1), (y + 2, xl),
        (y - d, xl), (y + d, xl), (y - d, xl + 1), (y + 2, xl + 1), (y + d, xl + 1),
    )
    for j, (yy, hh) in enumerate(spots):
        lanes = pl.ds(pl.multiple_of(((yy + 4) % 4 * 2 + hh % 2) * 128, 128), 128)
        cut = slice(j * 128, (j + 1) * 128)
        out[:, lanes] = (a[:, cut].astype(F32) + b[:, cut].astype(F32)).astype(BF)


def join(a, b):
    return pl.pallas_call(
        join_kernel,
        out_shape=jax.ShapeDtypeStruct(a.shape, BF),
        compiler_params=params(),
        cost_estimate=cost(a.size, 6 * a.size),
        name="join",
    )(a, b)


def finish_kernel(a, b, c, e, g0, g1, g2):
    for s, out in enumerate((g0, g1, g2)):
        total = a[s].astype(F32) + b[s].astype(F32) + c[s].astype(F32) + e[s].astype(F32)
        out[...] = total.T.astype(BF)


def finish(a, b, c, e):
    _, cols, depth = a.shape
    return pl.pallas_call(
        finish_kernel,
        out_shape=[jax.ShapeDtypeStruct((depth, cols), BF)] * 3,
        compiler_params=params(),
        cost_estimate=cost(4 * a.size, 10 * a.size),
        name="finish",
    )(a, b, c, e)


def body(low_state, mid_state, high_state, w_low, w_mid, w_high, kv_grad, loss_mask):
    states = (low_state, mid_state, high_state)
    w, mt = prepare((w_low, w_mid, w_high), kv_grad, loss_mask)
    a1 = send(w, Y1)
    a2 = send(w, Y2)
    x1 = send(w, XL)
    m_h = send(mt, XH)
    mt, *states = fence(mt, *states)
    states = load(*states)

    mt, m_h, *states = fence(mt, m_h, *states)
    pair = jnp.stack((mt, m_h))
    z1 = send(pair, Z1)
    z2 = send(pair, Z2)

    a1, a2, w, pair = fence(a1, a2, w, pair)
    a3 = send(a1, Y1)
    pair_o = send(pair, CORE)
    mine_a, theirs_a = forward(states, (w, a1))

    x1, z1, z2, pair_o, theirs_a, *states = fence(x1, z1, z2, pair_o, theirs_a, *states)
    b1 = send(x1, Y1)
    b3 = send(a3, XL)
    across = send(z1, Z1)
    z1_o = send(z1, CORE)
    z2_o = send(z2, CORE)
    mine_b, theirs_b = forward(states, (x1, a3))

    across, z1_o, z2_o, x1, theirs_b = fence(across, z1_o, z2_o, x1, theirs_b)
    across_o = send(across, CORE)
    b2 = send(x1, Y2)
    masked = (pair, z1, z2, across, pair_o, z1_o, z2_o, across_o)
    p2x, pmx, ppx, p0x = backward(states, masked, True, ("far", "back", "ahead", "here"))

    b1, p2x, pmx, ppx, p0x, pair = fence(b1, p2x, pmx, ppx, p0x, pair)
    masked = (pair, *masked[1:])
    e2 = send(pmx, Y2)
    e3 = send(ppx, Y1)
    e1 = send(p2x, XL)
    got_a = send(theirs_a, CORE)
    got_b = send(theirs_b, CORE)
    p2, pm, pp, p0 = backward(states, masked, False, ("far", "back", "ahead", "here"))

    got_a, got_b, p0, b1, a3 = fence(got_a, got_b, p0, b1, a3)
    sums = ((0, 0, 0, 0), (1, 0, 1, 0), (1, 1, 1, 1))
    q2a, qma, qpa, q0a = pick(sums, (mine_a, mine_b), (got_a, got_b))
    t3a = send(q2a, Z2)
    t2a = send(qpa, Z1)
    qma, b1, b3 = fence(qma, b1, b3)
    mine_c, theirs_c = forward(states, (a2, b1))
    mine_d, theirs_d = forward(states, (b3, b2))

    e1, e2, e3, t3a, t2a, theirs_c, theirs_d, p2, pm, pp, p0 = fence(
        e1, e2, e3, t3a, t2a, theirs_c, theirs_d, p2, pm, pp, p0
    )
    got_c = send(theirs_c, CORE)
    got_d = send(theirs_d, CORE)
    f3 = send(add(p2, e1), Y2)
    f2 = send(pp, Y1)
    fx = send(add(p0x, e2, e3), XL)
    sums = ((0, 1, 1, 0), (1, 0, 0, 1), (1, 1, 2, 1), (2, 0, 2, 0), (2, 1, 1, 1))
    q2b, qmb, qpb, q0b = pick(sums, (mine_a, mine_c, mine_d), (got_a, got_c, got_d))
    t3b = send(q2b, Z2)
    t2b = send(qpb, Z1)

    t3b, t2b, qma, qmb = fence(t3b, t2b, qma, qmb)
    t1 = send(pass_on(qma, t3a, qmb, t3b), Z2)
    f1 = send(add(pm, f3), Y2)
    kept, given = split(q0a, q0b, t1, t2a, t2b)
    got, *grads = fence(send(given, XH), *finish(p0, fx, f1, f2))
    return (join(kept, got), *grads)


def solution(mesh):
    in_specs = (
        P("grp", "tp"),
        P("grp", "tp"),
        P("grp", "tp"),
        P("tp", "grp"),
        P("tp", "grp"),
        P("tp", "grp"),
        P(("grp", "tp"), None),
        P(("grp", "tp")),
    )
    out_specs = (P(("grp", "tp"), None), P("tp", "grp"), P("tp", "grp"), P("tp", "grp"))
    return jax.shard_map(body, mesh=mesh, in_specs=in_specs, out_specs=out_specs, check_vma=False)
```

```python
import jax
import jax.numpy as jnp
from jax import lax
from jax.experimental import pallas as pl
from jax.experimental.pallas import tpu as pltpu
from jax.sharding import PartitionSpec as P

BF = jnp.bfloat16
F32 = jnp.float32
MIB = 1024 * 1024
LOAD_MIB = 38
GRP, TP = 8, 16
CHEAP = 1000
FULL = ("grp", "tp")


def full_perm(move):
    pairs = []
    for g in range(GRP):
        for t in range(TP):
            y, xl, z, xh, c = move(g // 2, g % 2, t // 4, t // 2 % 2, t % 2)
            pairs.append((g * TP + t, (y % 4 * 2 + xl % 2) * TP + z % 4 * 4 + xh % 2 * 2 + c % 2))
    return pairs


Y1 = full_perm(lambda y, xl, z, xh, c: (y + 1 - 2 * c, xl, z, xh, c))
Y2 = full_perm(lambda y, xl, z, xh, c: (y - 1 + 2 * c, xl, z, xh, c))
Z1 = full_perm(lambda y, xl, z, xh, c: (y, xl, z + 1 - 2 * c, xh, c))
Z2 = full_perm(lambda y, xl, z, xh, c: (y, xl, z - 1 + 2 * c, xh, c))
XL = full_perm(lambda y, xl, z, xh, c: (y, xl + 1, z, xh, c))
XH = full_perm(lambda y, xl, z, xh, c: (y, xl, z, xh + 1, c))
CORE = full_perm(lambda y, xl, z, xh, c: (y, xl, z, xh, c + 1))


def send(array, pairs):
    return lax.ppermute(array, FULL, pairs)


def add(*arrays):
    total = arrays[0].astype(F32)
    for array in arrays[1:]:
        total = total + array.astype(F32)
    return total.astype(BF)


def place():
    g = lax.axis_index("grp")
    t = lax.axis_index("tp")
    c = t % 2
    return g // 2, g % 2, t // 4, t // 2 % 2, c, 1 - 2 * c


def params(mib=8):
    return pltpu.CompilerParams(vmem_limit_bytes=mib * MIB)


def cost(flops, bytes_accessed):
    return pl.CostEstimate(flops=flops // CHEAP, bytes_accessed=bytes_accessed // CHEAP, transcendentals=0)


def fence(*arrays):
    return lax.optimization_barrier(arrays)


VMEM = pl.BlockSpec(memory_space=pltpu.VMEM)


def prepare_kernel(w0, w1, w2, grad_ref, mask_ref, w_ref, turned_ref, grad, mask, sems):
    depth = w0.shape[0]
    moves = [
        pltpu.make_async_copy(mask_ref, mask, sems.at[0]),
        pltpu.make_async_copy(grad_ref, grad, sems.at[1]),
    ]
    for i, w in enumerate((w0, w1, w2)):
        moves.append(pltpu.make_async_copy(w, w_ref.at[pl.ds(i * depth, depth), :], sems.at[2 + i]))
    for move in moves:
        move.start()
    moves[0].wait()
    moves[1].wait()
    turned_ref[...] = (grad[...].astype(F32).T * mask[...].astype(F32)).astype(BF)
    for move in moves[2:]:
        move.wait()


def prepare(weights, kv_grad, loss_mask):
    rows, cols = kv_grad.shape
    depth, width = weights[0].shape
    return pl.pallas_call(
        prepare_kernel,
        in_specs=[pl.BlockSpec(memory_space=pl.ANY)] * 5,
        out_specs=[VMEM] * 2,
        out_shape=[jax.ShapeDtypeStruct((3 * depth, width), BF), jax.ShapeDtypeStruct((cols, rows), BF)],
        scratch_shapes=[
            pltpu.VMEM((rows, cols), BF),
            pltpu.VMEM((1, rows), jnp.int32),
            pltpu.SemaphoreType.DMA((5,)),
        ],
        compiler_params=params(60),
        cost_estimate=cost(rows * cols, 4 * rows * cols + 12 * depth * width),
        name="prepare",
    )(*weights, kv_grad, loss_mask.reshape(1, rows))


def load_kernel(*refs):
    half = len(refs) // 2
    sems = refs[-1]
    moves = [pltpu.make_async_copy(refs[i], refs[half + i], sems.at[i]) for i in range(half)]
    for move in moves:
        move.start()
    for move in moves:
        move.wait()


def load(*arrays):
    count = len(arrays)
    return pl.pallas_call(
        load_kernel,
        in_specs=[pl.BlockSpec(memory_space=pl.ANY)] * count,
        out_specs=[VMEM] * count,
        out_shape=[jax.ShapeDtypeStruct(a.shape, BF) for a in arrays],
        scratch_shapes=[pltpu.SemaphoreType.DMA((count,))],
        compiler_params=params(LOAD_MIB),
        cost_estimate=cost(0, 4 * sum(a.size for a in arrays)),
        name="load",
    )(*arrays)


def forward_kernel(s0, s1, s2, wa, wb, mine_ref, theirs_ref, w_all):
    c = lax.axis_index("tp") % 2
    w_all[:, 0:128] = wa[...]
    w_all[:, 128:256] = wb[...]
    depth = s0.shape[1]
    total = jnp.dot(s0[...], w_all[0:depth, :], preferred_element_type=F32)
    total += jnp.dot(s1[...], w_all[depth:2 * depth, :], preferred_element_type=F32)
    total += jnp.dot(s2[...], w_all[2 * depth:3 * depth, :], preferred_element_type=F32)
    total = total.astype(BF)
    for z in range(4):
        for h in range(2):
            at = (z * 2 + h) * 256
            first = total[at:at + 128]
            second = total[at + 128:at + 256]
            mine_ref[z, h] = jnp.where(c == 0, first, second)
            theirs_ref[z, h] = jnp.where(c == 0, second, first)


def forward(states, blocks):
    tokens, depth = states[0].shape
    out = jax.ShapeDtypeStruct((4, 2, 128, 256), BF)

    return pl.pallas_call(
        forward_kernel,
        in_specs=[VMEM] * 5,
        out_specs=[VMEM] * 2,
        out_shape=[out, out],
        scratch_shapes=[pltpu.VMEM((3 * depth, 256), BF)],
        compiler_params=params(16),
        cost_estimate=cost(6 * tokens * depth * 256, 6 * tokens * depth + 8 * depth * 256),
        name="forward",
    )(*states, *blocks)


def backward_kernel(other, dests, refs):
    mine, theirs, (s0, s1, s2) = refs[:4], refs[4:8], refs[8:11]
    outs, turned = refs[11:-1], refs[-1]
    y, xl, z, xh, c, d = place()
    half = (xl + 1) % 2 if other else xl
    spots = {"far": y + 2, "back": y - d, "ahead": y + d, "here": y}
    for pieces, core in ((mine, c), (theirs, 1 - c)):
        way = 1 - 2 * core
        pair = ((z, xh), (z, xh + 1))
        back = ((z - way, xh), (z - way, xh + 1))
        ahead = ((z + way, xh), (z + way, xh + 1))
        across = ((z + 2, xh), (z + 2, xh + 1))
        for ref, j, (zz, hh) in (
            (ref, j, at) for ref, ats in zip(pieces, (pair, back, ahead, across)) for j, at in enumerate(ats)
        ):
            token = (zz + 4) % 4 * 4 + hh % 2 * 2 + core
            lanes = pl.ds(pl.multiple_of(token * 128, 128), 128)
            for r, dest in enumerate(dests):
                rows = pl.ds(pl.multiple_of(((spots[dest] + 4) % 4 * 2 + half) * 128, 128), 128)
                turned[r * 128:(r + 1) * 128, lanes] = ref[j, rows, :]

    @pl.loop(0, s0.shape[1] // 512)
    def _(i):
        cols = pl.ds(pl.multiple_of(i * 512, 512), 512)
        for s, state in enumerate((s0, s1, s2)):
            product = jnp.dot(turned[...], state[:, cols], preferred_element_type=F32) * (16384 ** -0.5)
            product = product.astype(BF)
            for r, out in enumerate(outs):
                out[s, :, cols] = product[r * 128:(r + 1) * 128]


def backward(states, masked, other, dests):
    tokens, depth = states[0].shape
    count = len(dests)
    out = jax.ShapeDtypeStruct((3, 128, depth), BF)

    def kernel(*refs):
        backward_kernel(other, dests, refs)

    return pl.pallas_call(
        kernel,
        in_specs=[VMEM] * 11,
        out_specs=[VMEM] * count,
        out_shape=[out] * count,
        scratch_shapes=[pltpu.VMEM((128 * count, tokens), BF)],
        compiler_params=params(16),
        cost_estimate=cost(6 * tokens * depth * 128 * count, 6 * tokens * depth + 16 * tokens * 256),
        name="backward",
    )(*masked, *states)


def pick_kernel(sums, refs):
    _, _, z, _, _, d = place()
    count = (len(refs) - 4) // 2
    mine, theirs = refs[:count], refs[count:2 * count]
    for out, zz in zip(refs[2 * count:], (z + 2, z - d, z + d, z)):
        k = (zz + 4) % 4
        for i, (m, m_half, t, t_half) in enumerate(sums):
            m_cut = slice(m_half * 128, m_half * 128 + 128)
            t_cut = slice(t_half * 128, t_half * 128 + 128)
            total = mine[m][k, :, :, m_cut].astype(F32) + theirs[t][k, :, :, t_cut].astype(F32)
            out[:, :, i * 128:(i + 1) * 128] = total.astype(BF)


def pick(sums, mine, theirs):
    size = sum(a.size for a in mine)
    out = jax.ShapeDtypeStruct((2, 128, 128 * len(sums)), BF)

    def kernel(*refs):
        pick_kernel(sums, refs)

    return pl.pallas_call(
        kernel,
        out_shape=[out] * 4,
        compiler_params=params(),
        cost_estimate=cost(size, 6 * size),
        name="pick",
    )(*mine, *theirs)


def split_kernel(a0, a1, b, c0, c1, mine, theirs):
    h = lax.axis_index("tp") // 2 % 2
    for out, k in ((mine, h), (theirs, (h + 1) % 2)):
        at = 0
        for a, c in ((a0, c0), (a1, c1)):
            cut = slice(at, at + a.shape[2])
            at += a.shape[2]
            out[:, cut] = (a[k].astype(F32) + b[k, :, cut].astype(F32) + c[k].astype(F32)).astype(BF)


def split(a0, a1, b, c0, c1):
    out = jax.ShapeDtypeStruct(b.shape[1:], BF)
    return pl.pallas_call(
        split_kernel,
        out_shape=[out] * 2,
        compiler_params=params(),
        cost_estimate=cost(2 * b.size, 8 * b.size),
        name="split",
    )(a0, a1, b, c0, c1)


def pass_kernel(qa, ta, qb, tb, out):
    at = 0
    for q, t in ((qa, ta), (qb, tb)):
        out[:, :, at:at + q.shape[2]] = (q[...].astype(F32) + t[...].astype(F32)).astype(BF)
        at += q.shape[2]


def pass_on(qa, ta, qb, tb):
    cols = qa.shape[2] + qb.shape[2]
    return pl.pallas_call(
        pass_kernel,
        out_shape=jax.ShapeDtypeStruct((*qa.shape[:2], cols), BF),
        compiler_params=params(),
        cost_estimate=cost(256 * cols, 1536 * cols),
        name="pass_on",
    )(qa, ta, qb, tb)


def join_kernel(a, b, out):
    y, xl, _, _, _, d = place()
    spots = (
        (y, xl), (y, xl + 1), (y + 2, xl),
        (y - d, xl), (y + d, xl), (y - d, xl + 1), (y + 2, xl + 1), (y + d, xl + 1),
    )
    for j, (yy, hh) in enumerate(spots):
        lanes = pl.ds(pl.multiple_of(((yy + 4) % 4 * 2 + hh % 2) * 128, 128), 128)
        cut = slice(j * 128, (j + 1) * 128)
        out[:, lanes] = (a[:, cut].astype(F32) + b[:, cut].astype(F32)).astype(BF)


def join(a, b):
    return pl.pallas_call(
        join_kernel,
        out_shape=jax.ShapeDtypeStruct(a.shape, BF),
        compiler_params=params(),
        cost_estimate=cost(a.size, 6 * a.size),
        name="join",
    )(a, b)


def finish_kernel(a, b, c, e, g0, g1, g2):
    for s, out in enumerate((g0, g1, g2)):
        total = a[s].astype(F32) + b[s].astype(F32) + c[s].astype(F32) + e[s].astype(F32)
        out[...] = total.T.astype(BF)


def finish(a, b, c, e):
    _, cols, depth = a.shape
    return pl.pallas_call(
        finish_kernel,
        out_shape=[jax.ShapeDtypeStruct((depth, cols), BF)] * 3,
        compiler_params=params(),
        cost_estimate=cost(4 * a.size, 10 * a.size),
        name="finish",
    )(a, b, c, e)


def body(low_state, mid_state, high_state, w_low, w_mid, w_high, kv_grad, loss_mask):
    states = (low_state, mid_state, high_state)
    w, mt = prepare((w_low, w_mid, w_high), kv_grad, loss_mask)
    a1 = send(w, Y1)
    a2 = send(w, Y2)
    x1 = send(w, XL)
    m_h = send(mt, XH)
    mt, *states = fence(mt, *states)
    states = load(*states)

    mt, m_h, *states = fence(mt, m_h, *states)
    pair = jnp.stack((mt, m_h))
    z1 = send(pair, Z1)
    z2 = send(pair, Z2)

    a1, a2, w, pair = fence(a1, a2, w, pair)
    a3 = send(a1, Y1)
    pair_o = send(pair, CORE)
    mine_a, theirs_a = forward(states, (w, a1))

    x1, z1, z2, pair_o, theirs_a, *states = fence(x1, z1, z2, pair_o, theirs_a, *states)
    b1 = send(x1, Y1)
    b3 = send(a3, XL)
    across = send(z1, Z1)
    z1_o = send(z1, CORE)
    z2_o = send(z2, CORE)
    mine_b, theirs_b = forward(states, (x1, a3))

    across, z1_o, z2_o, x1, theirs_b = fence(across, z1_o, z2_o, x1, theirs_b)
    across_o = send(across, CORE)
    b2 = send(x1, Y2)
    masked = (pair, z1, z2, across, pair_o, z1_o, z2_o, across_o)
    p2x, pmx, ppx, p0x = backward(states, masked, True, ("far", "back", "ahead", "here"))

    e2 = send(pmx, Y2)
    e3 = send(ppx, Y1)
    b1, b3, p2x, p0x, pair = fence(b1, b3, p2x, p0x, pair)
    masked = (pair, *masked[1:])
    e1 = send(p2x, XL)
    got_a = send(theirs_a, CORE)
    got_b = send(theirs_b, CORE)
    p2, pm, pp, p0 = backward(states, masked, False, ("far", "back", "ahead", "here"))

    got_a, got_b, p0, b1, a3 = fence(got_a, got_b, p0, b1, a3)
    sums = ((0, 0, 0, 0), (1, 0, 1, 0), (1, 1, 1, 1))
    q2a, qma, qpa, q0a = pick(sums, (mine_a, mine_b), (got_a, got_b))
    t3a = send(q2a, Z2)
    t2a = send(qpa, Z1)
    qma, b1, b3 = fence(qma, b1, b3)
    mine_c, theirs_c = forward(states, (a2, b1))
    mine_d, theirs_d = forward(states, (b3, b2))

    e1, e2, e3, t3a, t2a, theirs_c, theirs_d, p2, pm, pp, p0 = fence(
        e1, e2, e3, t3a, t2a, theirs_c, theirs_d, p2, pm, pp, p0
    )
    got_c = send(theirs_c, CORE)
    got_d = send(theirs_d, CORE)
    f3 = send(add(p2, e1), Y2)
    f2 = send(pp, Y1)
    fx = send(add(p0x, e2, e3), XL)
    sums = ((0, 1, 1, 0), (1, 0, 0, 1), (1, 1, 2, 1), (2, 0, 2, 0), (2, 1, 1, 1))
    q2b, qmb, qpb, q0b = pick(sums, (mine_a, mine_c, mine_d), (got_a, got_c, got_d))
    t3b = send(q2b, Z2)
    t2b = send(qpb, Z1)

    t3b, t2b, qma, qmb = fence(t3b, t2b, qma, qmb)
    t1 = send(pass_on(qma, t3a, qmb, t3b), Z2)
    f1 = send(add(pm, f3), Y2)
    kept, given = split(q0a, q0b, t1, t2a, t2b)
    got, *grads = fence(send(given, XH), *finish(p0, fx, f1, f2))
    return (join(kept, got), *grads)


def solution(mesh):
    in_specs = (
        P("grp", "tp"),
        P("grp", "tp"),
        P("grp", "tp"),
        P("tp", "grp"),
        P("tp", "grp"),
        P("tp", "grp"),
        P(("grp", "tp"), None),
        P(("grp", "tp")),
    )
    out_specs = (P(("grp", "tp"), None), P("tp", "grp"), P("tp", "grp"), P("tp", "grp"))
    return jax.shard_map(body, mesh=mesh, in_specs=in_specs, out_specs=out_specs, check_vma=False)
```
